256 devices in a mesh: group: 16 (over z, core), dev: 16 (over y, x).
Axes of the slice: x: 4, y: 4, z: 8, core: 2. Of those that a mesh axis runs over, the one named last changes fastest.
Arguments:
- rhs_fine: float32 [256, 256, 512], P('group', 'dev'), may hold values from -6 to 6
- diag_fine: float32 [256, 256, 512], P('group', 'dev'), may hold values from 2 to 4
- coup_fine: bfloat16 [26, 256, 256, 512], P(None, 'group', 'dev'), may hold values from 0.0039978027 to 0.06982422
- diag_mid: float32 [128, 128, 256], P('group', 'dev'), may hold values from 2 to 4
- coup_mid: bfloat16 [26, 128, 128, 256], P(None, 'group', 'dev'), may hold values from 0.0039978027 to 0.06982422
- diag_coarse: float32 [64, 64, 128], P('group', 'dev'), may hold values from 2 to 4
- coup_coarse: bfloat16 [26, 64, 64, 128], P(None, 'group', 'dev'), may hold values from 0.0039978027 to 0.06982422
- owner_map: int32 [16, 16, 16, 1], P('group', 'dev'), may hold values from 0 to 15; in each aligned block of 16 rows (0 to 15, 16 to 31, ..., all dimensions but the last counted through in order) at most 2 rows name the same one
- inverse_blocks: float32 [16, 16, 32, 128, 128], P('group', 'dev'), may hold values from -0.5 to 0.5
Outputs:
- fine_iterate: float32 [256, 256, 512], P('group', 'dev')
- mid_iterate: float32 [128, 128, 256], P('group', 'dev')
- coarse_correction: float32 [64, 64, 128], P('group', 'dev')
- coarse_residual: float32 [64, 64, 128], P('group', 'dev')
The draws below stay inside these ranges and needn't reach their ends.
Inputs may be any that keep to these rules, and one draw needn't show every extreme that they name: `owner_map`: owners lie in the block's own part group. On one device no owner is named by more than 2 of its 16 blocks, and in every draw some device names one owner exactly 2 times.
All inputs are finite; a program needn't handle non-finite values.
Results may differ from the reference program's by a relative error of at most 0.0003.
Values sent between devices are 32-bit elements; how exact they have to be, the bound alone decides.
No kernel may reach another device: no remote copies, remote signals or barrier semaphores. Data moves between devices by JAX's collectives and lax.ppermute only.
A program may use at most 128 MiB of HBM per device.

```python
import math
import jax
import jax.numpy as jnp
import numpy as np
from jax import lax

CX = 16
CY = 16
BLK = 128
NU = 3
NX = 256
NY = 256
NZ = 512
NB = 16
CAP = 2
SLOTS = 32
N_GROUP = 16
N_DEV = 16


def block_scale(own_key, extent, shards, smallest, top_value):
    loudness = 1.0
    for dim, parts in shards:
        draws = jax.random.uniform(jax.random.fold_in(jax.random.fold_in(own_key, 6), dim), (parts,), jnp.float32, smallest / len(shards), top_value / len(shards))
        loudness = loudness * jnp.repeat(jnp.exp(draws), extent[dim] // parts).reshape((-1,) + (1,) * (len(extent) - 1 - dim))
    return loudness


def assign_block(key, own, number, rows, count, top, bound, lean):
    sequence = jax.random.permutation(key, count)
    crowded, usual = load_shares(count, rows * top, bound, lean, True), load_shares(count, rows * top, bound, lean, False)
    places = jnp.arange(count)

    def named(tallies, offset_by):
        used = int((tallies > 0).sum())
        fixed = max(1, used // 4)
        moved = fixed + (places - fixed + offset_by * (used - fixed)) % max(1, count - fixed)
        return jnp.zeros((count,), jnp.int32).at[sequence[jnp.where(places < fixed, places, moved)]].set(jnp.asarray(tallies, jnp.int32))

    tallies = jnp.where(number % 4 == 0, named(crowded, number // 4), named(usual, number - number // 4 - 1))
    mixed = jax.random.permutation(jax.random.fold_in(own, 3), count)
    donor, sink = mixed[0:count // 2 * 2:2], mixed[1:count // 2 * 2:2]
    slack = jnp.minimum(tallies[donor] - 1, bound - tallies[sink]) // 2
    slack = jnp.where((donor == sequence[0]) | (sink == sequence[0]) | (tallies[sink] == 0), 0, jnp.maximum(slack, 0))
    moved = jax.random.randint(jax.random.fold_in(own, 4), (count // 2,), 0, 1 << 20) % (slack + 1)
    tallies = tallies.at[donor].add(-moved).at[sink].add(moved)
    items = jnp.searchsorted(jnp.cumsum(tallies), jnp.arange(rows * top), side="right").astype(jnp.int32)
    table = items.reshape(top, rows).T
    table = table[jax.random.permutation(jax.random.fold_in(own, 1), rows)]
    offset_by = jax.random.randint(jax.random.fold_in(own, 2), (rows, 1), 0, top)
    return jnp.take_along_axis(table, (jnp.arange(top)[None, :] + offset_by) % top, axis=1)


def load_shares(count, total, most, slope, full):
    portions = [(1 << 20) // math.isqrt(standing ** slope) + 1 for standing in range(1, count + 1)]
    largest = most if full else min(most, max(-(-total // count), total * portions[0] // sum(portions)))
    least = 1 if total - largest >= count - 1 else 0
    given, rest = [largest] + [least] * (count - 1), total - largest - least * (count - 1)
    while rest > 0:
        free = [i for i in range(1, count) if given[i] < largest] or [i for i in range(1, count) if given[i] < most]
        whole, budget = sum([portions[i] for i in free]), rest
        for i in free:
            extra = min(most - given[i], max(1, budget * portions[i] // whole), rest)
            given[i] = given[i] + extra
            rest = rest - extra
    return np.array(given)


def scatter_about(key, shape, scale, most, pieces=(), kind=jnp.bfloat16):
    array = jax.random.normal(key, shape, jnp.float32) * scale
    if len(pieces) > 0:
        array = block_scale(key, shape, pieces, -0.22, 0.18) * array
    return jnp.clip(array, min=-most, max=most).astype(kind)


def setup_inputs(seed: int = 0) -> dict:
    key_of = jax.random.split(jax.random.key(seed), 10)
    rhs_fine = scatter_about(key_of[0], (NX, NY, NZ), 1.0, 6.0, ((0, 16), (1, 16)), jnp.float32)
    diag_fine = jnp.clip(2.0 + 2.0 * jax.random.uniform(key_of[1], (NX, NY, NZ), jnp.float32) ** block_scale(key_of[1], (NX, NY, NZ), ((0, 16), (1, 16)), -0.2, 0.2), 2.0, 4.0)
    coup_fine = jnp.clip(jnp.exp(math.log(0.06982422) - 2.860236 * jax.random.uniform(key_of[2], (26, NX, NY, NZ), jnp.float32) ** block_scale(key_of[2], (26, NX, NY, NZ), ((1, 16), (2, 16)), -0.2, 0.2)), 0.0039978027, 0.06982422).astype(jnp.bfloat16)
    diag_mid = jnp.clip(2.0 + 2.0 * jax.random.uniform(key_of[3], (NX // 2, NY // 2, NZ // 2), jnp.float32) ** block_scale(key_of[3], (NX // 2, NY // 2, NZ // 2), ((0, 16), (1, 16)), -0.2, 0.2), 2.0, 4.0)
    coup_mid = jnp.clip(jnp.exp(math.log(0.06982422) - 2.860236 * jax.random.uniform(key_of[4], (26, NX // 2, NY // 2, NZ // 2), jnp.float32) ** block_scale(key_of[4], (26, NX // 2, NY // 2, NZ // 2), ((1, 16), (2, 16)), -0.2, 0.2)), 0.0039978027, 0.06982422).astype(jnp.bfloat16)
    diag_coarse = jnp.clip(2.0 + 2.0 * jax.random.uniform(key_of[5], (NX // 4, NY // 4, NZ // 4), jnp.float32) ** block_scale(key_of[5], (NX // 4, NY // 4, NZ // 4), ((0, 16), (1, 16)), -0.2, 0.2), 2.0, 4.0)
    coup_coarse = jnp.clip(jnp.exp(math.log(0.06982422) - 2.860236 * jax.random.uniform(key_of[6], (26, NX // 4, NY // 4, NZ // 4), jnp.float32) ** block_scale(key_of[6], (26, NX // 4, NY // 4, NZ // 4), ((1, 16), (2, 16)), -0.2, 0.2)), 0.0039978027, 0.06982422).astype(jnp.bfloat16)
    owner_map_keys = jax.random.split(jax.random.fold_in(key_of[7], 1), N_GROUP * N_DEV * NB // NB)
    owner_map_turns = jax.random.permutation(jax.random.fold_in(key_of[7], 3), N_GROUP * N_DEV * NB // NB)
    owner_map = jax.vmap(lambda own, number: assign_block(jax.random.fold_in(key_of[7], 2), own, number, NB, N_DEV, 1, CAP, 2))(owner_map_keys, owner_map_turns).reshape((N_GROUP, N_DEV, NB, 1))
    inverse_blocks = scatter_about(key_of[8], (N_GROUP, N_DEV, SLOTS, BLK, BLK), BLK ** -0.5, 0.5, ((0, 16), (1, 16)), jnp.float32)
    return {"rhs_fine": rhs_fine, "diag_fine": diag_fine, "coup_fine": coup_fine, "diag_mid": diag_mid, "coup_mid": coup_mid, "diag_coarse": diag_coarse, "coup_coarse": coup_coarse, "owner_map": owner_map, "inverse_blocks": inverse_blocks}


OMEGA = 0.8
HALVING = 0.5
OFFSETS = [(shift_x, shift_y, shift_z) for shift_x in (-1, 0, 1) for shift_y in (-1, 0, 1) for shift_z in (-1, 0, 1) if (shift_x, shift_y, shift_z) != (0, 0, 0)]


def stencil(padded, values, diagonal, couplings):
    length_x, length_y, length_z = values.shape[-3:]
    result = diagonal * values
    for position, (shift_x, shift_y, shift_z) in enumerate(OFFSETS):
        beside = padded[..., 1 + shift_x:1 + shift_x + length_x, 1 + shift_y:1 + shift_y + length_y, 1 + shift_z:1 + shift_z + length_z]
        result = result - couplings[..., position, :, :, :].astype(jnp.float32) * beside
    return result


def frame_zero(values):
    widths = [(0, 0)] * (values.ndim - 3) + [(1, 1)] * 3
    return jnp.pad(values, widths)


def smooth_level(source, diagonal, couplings, framer):
    iterate = OMEGA * source / diagonal
    for sweep_index in range(NU - 1):
        iterate = iterate + OMEGA * (source - stencil(framer(iterate), iterate, diagonal, couplings)) / diagonal
    leftover = source - stencil(framer(iterate), iterate, diagonal, couplings)
    return iterate, leftover


def coarsen(values):
    length_x, length_y, length_z = values.shape
    grouped = values.reshape(length_x // 2, 2, length_y // 2, 2, length_z // 2, 2)
    return HALVING * jnp.sum(grouped, axis=(1, 3, 5))


def block_ranks(owners):
    blocks_count = owners.shape[-1]
    same_owner = owners[..., :, None] == owners[..., None, :]
    earlier = jnp.arange(blocks_count)[None, :] < jnp.arange(blocks_count)[:, None]
    return jnp.sum((same_owner & earlier).astype(jnp.int32), axis=-1).astype(jnp.int32)


def reference(rhs_fine, diag_fine, coup_fine, diag_mid, coup_mid, diag_coarse, coup_coarse, owner_map, inverse_blocks):
    fine_iterate, fine_left = smooth_level(rhs_fine, diag_fine, coup_fine, frame_zero)
    mid_iterate, mid_left = smooth_level(coarsen(fine_left), diag_mid, coup_mid, frame_zero)
    coarse_source = coarsen(mid_left)
    quarter_x = CX // 4
    quarter_y = CY // 4
    block_z = BLK // (quarter_x * quarter_y)

    def to_blocks(values):
        return values.reshape(N_GROUP, quarter_x, N_DEV, quarter_y, NB, block_z).transpose(0, 2, 4, 1, 3, 5)

    def from_blocks(blocks):
        return blocks.transpose(0, 3, 1, 4, 2, 5).reshape(N_GROUP * quarter_x, N_DEV * quarter_y, NB * block_z)

    source_blocks = to_blocks(coarse_source)
    diag_blocks = to_blocks(diag_coarse)
    coup_blocks = coup_coarse.reshape(26, N_GROUP, quarter_x, N_DEV, quarter_y, NB, block_z).transpose(1, 3, 5, 0, 2, 4, 6)
    owners = owner_map[..., 0]
    ranks = block_ranks(owners)
    slot_index = (jnp.arange(N_DEV, dtype=jnp.int32)[:, None] * CAP + ranks).astype(jnp.int32)

    def per_group(inputs):
        inverse_group, owner_group, slot_group, source_group = inputs
        matrices = inverse_group[owner_group, slot_group]
        flat_source = source_group.reshape(N_DEV, NB, BLK)
        return jnp.einsum('snij,snj->sni', matrices, flat_source, precision=lax.Precision.HIGHEST)

    correction = lax.map(per_group, (inverse_blocks, owners, slot_index, source_blocks))
    correction = correction.reshape(source_blocks.shape)
    leftover = source_blocks - stencil(frame_zero(correction), correction, diag_blocks, coup_blocks)
    return fine_iterate, mid_iterate, from_blocks(correction), from_blocks(leftover)
```

```python
import functools

import jax
import jax.numpy as jnp
from jax import lax
from jax.experimental import pallas as pl
from jax.experimental.pallas import tpu as pltpu
from jax.sharding import PartitionSpec as P

OMEGA = 0.8
HALVING = 0.5
OFFSETS = [
    (a, b, c)
    for a in (-1, 0, 1)
    for b in (-1, 0, 1)
    for c in (-1, 0, 1)
    if (a, b, c) != (0, 0, 0)
]
TO_YLO = [OFFSETS.index((a, -1, c)) for a in (-1, 0, 1) for c in (-1, 0, 1)]
TO_YHI = [OFFSETS.index((a, 1, c)) for a in (-1, 0, 1) for c in (-1, 0, 1)]
F32 = jnp.float32
HIGHEST = lax.Precision.HIGHEST
VMEM_LIMIT = 20 * 1024 * 1024
XB = 4
WIDE = 3
X_LO, X_HI, Y_LO, Y_HI, X_ODD, Y_ODD = range(6)
LONG = 30_000_000_000
VMEM = pl.BlockSpec(memory_space=pltpu.VMEM)
SMEM = pl.BlockSpec(memory_space=pltpu.SMEM)


def sds(shape, dtype=F32):
    return jax.ShapeDtypeStruct(shape, dtype)


def iota(shape, dim):
    return lax.broadcasted_iota(jnp.int32, shape, dim)


def shift_z(v, c):
    if c == 0:
        return v
    n, dim = v.shape[-1], v.ndim - 1
    edge = 0 if c < 0 else n - 1
    return jnp.where(iota(v.shape, dim) == edge, 0.0, pltpu.roll(v, (-c) % n, dim))


def shift_y(v, b):
    if b == 0:
        return v
    n, dim = v.shape[-2], v.ndim - 2
    edge = 0 if b < 0 else n - 1
    return jnp.where(iota(v.shape, dim) == edge, 0.0, pltpu.roll(v, (-b) % n, dim))


def pair_sum_right(n, scale):
    return jnp.where((iota((n, n // 2), 0) >> 1) == iota((n, n // 2), 1), scale, 0.0).astype(F32)


def pair_sum_left(n):
    return jnp.where((iota((n // 2, n), 1) >> 1) == iota((n // 2, n), 0), 1.0, 0.0).astype(F32)


def dot(a, b):
    return jnp.dot(a, b, precision=HIGHEST, preferred_element_type=F32)


def put_versions(s_ref, x, layer):
    for c in (-1, 0, 1):
        along = shift_z(layer, c)
        for b in (-1, 0, 1):
            s_ref[(b + 1) * 3 + c + 1, x + 1] = shift_y(along, b)


def neighbours(w_ref, s_ref, first, at):
    total = [None] * XB
    for b in (-1, 0, 1):
        for c in (-1, 0, 1):
            k = (b + 1) * 3 + c + 1
            layers = [s_ref[k, first + r, :, at] for r in range(XB + 2)]
            for a in (-1, 0, 1):
                if (a, b, c) == (0, 0, 0):
                    continue
                o = OFFSETS.index((a, b, c))
                for i in range(XB):
                    term = w_ref[o, first + i, :, at].astype(F32) * layers[i + 1 + a]
                    total[i] = term if total[i] is None else total[i] + term
    return total


def lane_chunks(n):
    return [slice(k, k + 128) for k in range(0, n, 128)]


def zero_rims(s_ref):
    for edge in (0, s_ref.shape[1] - 1):
        for k in range(9):
            s_ref[k, edge] = jnp.zeros(s_ref.shape[2:], F32)


def patched(v_ref, new, x, last):
    xlo, xhi, ylo, yhi = new
    layer = v_ref[x]
    row = iota(layer.shape, 0)
    layer = jnp.where(row == 0, ylo[pl.ds(x, 1), :], layer)
    layer = jnp.where(row == layer.shape[0] - 1, yhi[pl.ds(x, 1), :], layer)
    layer = jnp.where(x == 0, xlo[...], layer)
    return jnp.where(x == last, xhi[...], layer)


def put_faces(faces_ref, v_ref):
    nx, ny = v_ref.shape[:2]
    faces_ref[0] = v_ref[0]
    faces_ref[1] = v_ref[nx - 1]
    for x in range(nx):
        faces_ref[2, x : x + 1, :] = v_ref[x, 0:1, :]
        faces_ref[3, x : x + 1, :] = v_ref[x, ny - 1 : ny, :]


def put_next(v_ref, start_ref, q_ref, w_ref, s_ref, j):
    for at in lane_chunks(v_ref.shape[2]):
        for i, total in enumerate(neighbours(w_ref, s_ref, j * XB, at)):
            x = j * XB + i
            centre = (1.0 - OMEGA) * s_ref[4, x + 1, :, at]
            v_ref[x, :, at] = centre + start_ref[x, :, at] + q_ref[x, :, at] * total


def fine_start(flags, f_ref, d_ref, start_ref, q_ref, x_even, x_odd, ylo, yhi):
    nx, ny = f_ref.shape[:2]

    @pl.loop(0, nx)
    def _(x):
        q = OMEGA / d_ref[x]
        q_ref[x] = q
        start_ref[x] = q * f_ref[x]

    put_both(flags[X_ODD] > 0, x_even, x_odd, slice(None), start_ref[0], start_ref[nx - 1])
    for x in range(nx):
        ylo[x : x + 1, :] = start_ref[x, 0:1, :]
        yhi[x : x + 1, :] = start_ref[x, ny - 1 : ny, :]


def fine_first(
    start_ref, q_ref, w_ref, v_ref, faces_ref, qfaces_ref, wfaces_ref, s_ref, wy_ref
):
    nx, ny = v_ref.shape[:2]
    zero_rims(s_ref)

    @pl.loop(0, nx)
    def _(x):
        put_versions(s_ref, x, start_ref[x])

    @pl.loop(0, nx // XB)
    def _(j):
        put_next(v_ref, start_ref, q_ref, w_ref, s_ref, j)
        for i in range(XB):
            x = j * XB + i
            for k in range(9):
                wy_ref[0, k, pl.ds(x, 1), :] = w_ref[TO_YLO[k], x].astype(F32)[0:1, :]
                wy_ref[1, k, pl.ds(x, 1), :] = w_ref[TO_YHI[k], x].astype(F32)[ny - 1 : ny, :]

    wfaces_ref[0] = w_ref[0:9, 0]
    wfaces_ref[1] = w_ref[17:26, nx - 1]
    for k in range(9):
        wfaces_ref[2, k] = wy_ref[0, k].astype(wfaces_ref.dtype)
        wfaces_ref[3, k] = wy_ref[1, k].astype(wfaces_ref.dtype)
    put_faces(faces_ref, v_ref)
    put_faces(qfaces_ref, q_ref)


def fine_next(v_ref, xlo, xhi, ylo, yhi, start_ref, q_ref, w_ref, out_ref, faces_ref, s_ref):
    nx = v_ref.shape[0]
    zero_rims(s_ref)

    @pl.loop(0, nx)
    def _(x):
        put_versions(s_ref, x, patched(v_ref, (xlo, xhi, ylo, yhi), x, nx - 1))

    @pl.loop(0, nx // XB)
    def _(j):
        put_next(out_ref, start_ref, q_ref, w_ref, s_ref, j)

    put_faces(faces_ref, out_ref)


def fine_last(v_ref, xlo, xhi, ylo, yhi, start_ref, q_ref, w_ref, out_ref, g_ref, s_ref, p_ref):
    nx, ny, nz = v_ref.shape
    zero_rims(s_ref)

    @pl.loop(0, nx)
    def _(x):
        layer = patched(v_ref, (xlo, xhi, ylo, yhi), x, nx - 1)
        out_ref[x] = layer
        put_versions(s_ref, x, layer)

    @pl.loop(0, nx // XB)
    def _(j):
        for at in lane_chunks(nz):
            total = neighbours(w_ref, s_ref, j * XB, at)
            for i in range(XB):
                x = j * XB + i
                own = start_ref[x, :, at] - OMEGA * s_ref[4, x + 1, :, at]
                total[i] = total[i] + own / q_ref[x, :, at]
            for i in range(0, XB, 2):
                row = pl.multiple_of((j * (XB // 2) + i // 2) * ny, ny)
                p_ref[pl.ds(row, ny), at] = total[i] + total[i + 1]

    rows = dot(pair_sum_left(nx // 2 * ny), p_ref[...])
    g_ref[...] = dot(rows, pair_sum_right(nz, HALVING)).reshape(g_ref.shape)


def sides(flags, even, odd, lo, hi, parity):
    at_odd = flags[parity] > 0
    below = jnp.where(at_odd, even, odd)
    above = jnp.where(at_odd, odd, even)
    return jnp.where(flags[lo] > 0, below, 0.0), jnp.where(flags[hi] > 0, above, 0.0)


def halo_terms(flags, x_even, x_odd, y_even, y_odd, w_ref):
    xs, ys = [], []
    n = x_even.shape[0]
    x_sides = sides(flags, x_even[...], x_odd[...], X_LO, X_HI, X_ODD)
    y_sides = sides(flags, y_even[...], y_odd[...], Y_LO, Y_HI, Y_ODD)
    for side, halo in enumerate(x_sides):
        total = None
        for c in (-1, 0, 1):
            along = shift_z(halo, c)
            for b in (-1, 0, 1):
                term = w_ref[side, (b + 1) * 3 + c + 1].astype(F32) * shift_y(along, b)
                total = term if total is None else total + term
        xs.append(total)
    for side, halo in enumerate(y_sides):
        total = None
        for c in (-1, 0, 1):
            along = shift_z(halo, c)
            for a in (-1, 0, 1):
                term = w_ref[2 + side, (a + 1) * 3 + c + 1].astype(F32) * along[1 + a : 1 + a + n]
                total = term if total is None else total + term
        ys.append(total)
    return xs, ys


def fine_halo(flags, x_even, x_odd, y_even, y_odd, w_ref, faces_ref, q_ref, *outs):
    xs, ys = halo_terms(flags, x_even, x_odd, y_even, y_odd, w_ref)
    n = xs[0].shape[0]
    row = iota(xs[0].shape, 0)

    def crossed(own, others, place):
        own = jnp.where(row == 0, own + others[0][place : place + 1], own)
        return jnp.where(row == n - 1, own + others[1][place : place + 1], own)

    sums = [
        crossed(xs[0], ys, 0),
        crossed(xs[1], ys, n - 1),
        crossed(ys[0], xs, 0),
        crossed(ys[1], xs, n - 1),
    ]
    new = [faces_ref[k] + q_ref[k] * sums[k] for k in range(4)]
    for k in range(4):
        outs[k][...] = new[k]
    at_odd = flags[X_ODD] > 0
    outs[4][...] = jnp.where(at_odd, new[0], new[1])
    outs[5][...] = jnp.where(at_odd, new[1], new[0])


def fine_halo_last(
    flags, x_even, x_odd, y_even, y_odd, w_ref, g_ref, f_ref, to_even, to_odd, t_ref
):
    xs, ys = halo_terms(flags, x_even, x_odd, y_even, y_odd, w_ref)
    n, nz = xs[0].shape
    for k, part in enumerate(xs + ys):
        t_ref[k * n : (k + 1) * n, :] = part
    rows = dot(pair_sum_left(4 * n), t_ref[...])
    half = n // 2
    coarse = dot(rows, pair_sum_right(nz, HALVING))
    row = iota((half, nz // 2), 0)
    for i in range(half):
        total = g_ref[i]
        total = total + jnp.where(row == 0, coarse[2 * half + i : 2 * half + i + 1], 0.0)
        total = total + jnp.where(row == half - 1, coarse[3 * half + i : 3 * half + i + 1], 0.0)
        if i == 0:
            total = total + coarse[0:half]
        if i == half - 1:
            total = total + coarse[half : 2 * half]
        f_ref[i] = total
    at_odd = flags[X_ODD] > 0
    for k in range(WIDE):
        lo, hi = f_ref[k], f_ref[half - WIDE + k]
        to_even[k] = jnp.where(at_odd, lo, hi)
        to_odd[k] = jnp.where(at_odd, hi, lo)


def put_both(at_odd, even_ref, odd_ref, index, lo, hi):
    even_ref[index] = jnp.where(at_odd, lo, hi)
    odd_ref[index] = jnp.where(at_odd, hi, lo)


def mid_pack(flags, w_ref, d_ref, x_even, x_odd):
    nx = d_ref.shape[0]
    at_odd = flags[X_ODD] > 0

    @pl.loop(0, 26)
    def _(o):
        for k in range(2):
            lo, hi = w_ref[o, k].astype(F32), w_ref[o, nx - 2 + k].astype(F32)
            put_both(at_odd, x_even, x_odd, o * 2 + k, lo, hi)

    for k in range(WIDE):
        put_both(at_odd, x_even, x_odd, 52 + k, d_ref[k], d_ref[nx - WIDE + k])


def mid_assemble(flags, w_ref, d_ref, x_even, x_odd, w_out, q_out):
    nx = d_ref.shape[0]
    at_odd = flags[X_ODD] > 0

    def beyond(index, below):
        first, second = (x_even, x_odd) if below else (x_odd, x_even)
        return jnp.where(at_odd, first[index], second[index])

    @pl.loop(0, 26)
    def _(o):
        for x in range(nx):
            w_out[o, x + 2] = w_ref[o, x]
        for k in range(2):
            w_out[o, k] = beyond(o * 2 + k, True).astype(w_out.dtype)
            w_out[o, nx + 2 + k] = beyond(o * 2 + k, False).astype(w_out.dtype)

    for x in range(nx):
        q_out[x + WIDE] = OMEGA / d_ref[x]
    for k in range(WIDE):
        q_out[k] = OMEGA / beyond(52 + k, True)
        q_out[nx + WIDE + k] = OMEGA / beyond(52 + k, False)


def mid_start(flags, f_ref, e_ref, o_ref, q_ref, start_ref, y_even, y_odd):
    nx, ny = f_ref.shape[:2]
    x_odd, y_is_odd = flags[X_ODD] > 0, flags[Y_ODD] > 0
    for r in range(nx + 2 * WIDE):
        if r < WIDE:
            f = jnp.where(x_odd, e_ref[r], o_ref[r])
            f = jnp.where(flags[X_LO] > 0, f, 0.0)
        elif r >= nx + WIDE:
            k = r - nx - WIDE
            f = jnp.where(x_odd, o_ref[k], e_ref[k])
            f = jnp.where(flags[X_HI] > 0, f, 0.0)
        else:
            f = f_ref[r - WIDE]
        start = q_ref[r] * f
        start_ref[r] = start
        index = (slice(r, r + 1), slice(None))
        put_both(y_is_odd, y_even, y_odd, index, start[0:1], start[ny - 1 : ny])


def mid_neighbours(flags, v_ref, y_even, y_odd, w_ref, s_ref, reach):
    ny = v_ref.shape[1]
    y_lo, y_hi = sides(flags, y_even[...], y_odd[...], Y_LO, Y_HI, Y_ODD)
    row = iota(v_ref.shape[1:], 0)
    for r in range(v_ref.shape[0]):
        layer = v_ref[r]
        below = jnp.where(row == 0, y_lo[r : r + 1], pltpu.roll(layer, 1, 0))
        above = jnp.where(row == ny - 1, y_hi[r : r + 1], pltpu.roll(layer, ny - 1, 0))
        for b, moved in enumerate((below, layer, above)):
            for c in (-1, 0, 1):
                s_ref[b * 3 + c + 1, r] = shift_z(moved, c)

    def neighbours_of(x):
        total = None
        for o, (a, b, c) in enumerate(OFFSETS):
            term = w_ref[o, x + 2].astype(F32) * s_ref[(b + 1) * 3 + c + 1, x + a + reach]
            total = term if total is None else total + term
        return total

    return neighbours_of


def mid_next(
    reach, flags, v_ref, y_even, y_odd, start_ref, q_ref, w_ref, out_ref, to_even, to_odd, s_ref
):
    nx, ny = q_ref.shape[0] - 2 * WIDE, q_ref.shape[1]
    layers = range(1 - reach, nx + reach - 1)
    total = mid_neighbours(flags, v_ref, y_even, y_odd, w_ref, s_ref, reach)
    for k, x in enumerate(layers):
        new = (1.0 - OMEGA) * v_ref[k + 1] + start_ref[x + WIDE] + q_ref[x + WIDE] * total(x)
        if x < 0:
            new = jnp.where(flags[X_LO] > 0, new, 0.0)
        if x >= nx:
            new = jnp.where(flags[X_HI] > 0, new, 0.0)
        out_ref[k] = new
        index = (slice(k, k + 1), slice(None))
        put_both(flags[Y_ODD] > 0, to_even, to_odd, index, new[0:1], new[ny - 1 : ny])


def swap_blocks(values):
    n, lanes = values.shape
    width = lanes // n
    wide = jnp.broadcast_to(values[None], (n, n, lanes))
    wide = jnp.where(iota(wide.shape, 2) // width == iota(wide.shape, 0), wide, 0.0)
    spread = jnp.where(
        iota((lanes, lanes), 0) % width == iota((lanes, lanes), 1) % width, 1.0, 0.0
    ).astype(F32)
    moved = dot(wide.reshape(n * n, lanes), spread).reshape(n, n, lanes)
    moved = jnp.where(iota(moved.shape, 2) // width == iota(moved.shape, 1), moved, 0.0)
    return jnp.sum(moved, axis=1)


def mid_last(
    flags,
    places,
    v_ref,
    y_even,
    y_odd,
    f_ref,
    d_ref,
    w_ref,
    mid_out,
    src_out,
    slot_out,
    s_ref,
    p_ref,
):
    nx, ny, nz = f_ref.shape
    total = mid_neighbours(flags, v_ref, y_even, y_odd, w_ref, s_ref, 1)
    left = []
    for x in range(nx):
        mid_out[x] = v_ref[x + 1]
        left.append(f_ref[x] - d_ref[x] * v_ref[x + 1] + total(x))
    for i in range(nx // 2):
        p_ref[i * ny : (i + 1) * ny, :] = left[2 * i] + left[2 * i + 1]
    rows = dot(pair_sum_left(nx // 2 * ny), p_ref[...])
    source = dot(rows, pair_sum_right(nz, HALVING))
    src_out[...] = source
    blocked = swap_blocks(source)
    slot_out[...] = jnp.zeros(slot_out.shape, F32)
    for k in range(blocked.shape[0]):
        slot_out[pl.ds(places[k], 1), :] = blocked[k : k + 1]


def solve_blocks(m_ref, a_ref, out_ref):
    slots, cells = a_ref.shape
    lane = iota((cells, cells), 1)
    columns = jnp.zeros((cells, cells), F32)
    for q in range(slots):
        product = jnp.sum(m_ref[q] * a_ref[q : q + 1, :], axis=1, keepdims=True)
        columns = jnp.where(lane == q, product, columns)
    out_ref[...] = columns.T[0:slots]


def finish(places, back_ref, src_ref, dc_ref, wc_ref, cor_out, res_out, c_ref):
    blocks, cells = c_ref.shape
    nx, half = cor_out.shape[:2]
    rows = nx * half
    for k in range(blocks):
        c_ref[k : k + 1, :] = back_ref[pl.ds(places[k], 1), :]
    correction = swap_blocks(c_ref[...])
    source = src_ref[...]
    grid_row = iota(source.shape, 0)
    width = cells // blocks
    zpos = iota(source.shape, 1) % width
    residual = source - dc_ref[...] * correction
    for o, (a, b, c) in enumerate(OFFSETS):
        moved = correction
        if c:
            moved = pltpu.roll(moved, (-c) % cells, 1)
            moved = jnp.where(zpos == (0 if c < 0 else width - 1), 0.0, moved)
        if a or b:
            moved = pltpu.roll(moved, (-(a * half + b)) % rows, 0)
            y, x = grid_row % half + b, grid_row // half + a
            ok = (y >= 0) & (y < half) & (x >= 0) & (x < nx)
            moved = jnp.where(ok, moved, 0.0)
        residual = residual + wc_ref[o].astype(F32) * moved
    for x in range(nx):
        cor_out[x] = correction[x * half : (x + 1) * half]
        res_out[x] = residual[x * half : (x + 1) * half]


def block_ranks(owners):
    same = owners[:, None] == owners[None, :]
    count = owners.shape[0]
    earlier = jnp.arange(count)[None, :] < jnp.arange(count)[:, None]
    return jnp.sum((same & earlier).astype(jnp.int32), axis=-1)


def call(body, outs, ins=None, **more):
    flops = more.pop("flops", 1_000_000)
    size = more.pop("size", 1_000_000)
    limit = more.pop("limit", VMEM_LIMIT)
    return pl.pallas_call(
        body,
        out_shape=outs,
        cost_estimate=pl.CostEstimate(flops=flops, bytes_accessed=size, transcendentals=0),
        compiler_params=pltpu.CompilerParams(vmem_limit_bytes=limit),
        **more,
    )


def pairs(axis):
    size = lax.axis_size(axis)
    even = [(i, i ^ 1) for i in range(size)]
    odd = [(i, (i + 1) % size if i % 2 else (i - 1) % size) for i in range(size)]
    return even, odd


def exchange(axis, to_even, to_odd):
    even, odd = pairs(axis)
    return lax.ppermute(to_even, axis, even), lax.ppermute(to_odd, axis, odd)


def shards(
    rhs_fine,
    diag_fine,
    coup_fine,
    diag_mid,
    coup_mid,
    diag_coarse,
    coup_coarse,
    owner_map,
    inverse_blocks,
):
    nx, ny, nz = rhs_fine.shape
    g, d = lax.axis_index("group"), lax.axis_index("dev")
    n_group, n_dev = lax.axis_size("group"), lax.axis_size("dev")
    flags = jnp.stack([g > 0, g < n_group - 1, d > 0, d < n_dev - 1, g % 2 > 0, d % 2 > 0])
    slots, cells = inverse_blocks.shape[2], inverse_blocks.shape[3]
    owners = owner_map.reshape(-1)
    places = owners * (slots // n_dev) + block_ranks(owners)
    flags = lax.optimization_barrier(flags.astype(jnp.int32))

    def on(place):
        return flags[place] > 0

    def by_parity(parity, lo, hi):
        return jnp.where(on(parity), lo, hi), jnp.where(on(parity), hi, lo)

    scratch = [pltpu.VMEM((9, nx + 2, ny, nz), F32)]
    fine = sds((nx, ny, nz))
    faces = sds((4, ny, nz))
    heavy = dict(flops=60 * nx * ny * nz, size=coup_fine.size * 2 + 4 * rhs_fine.size * 4)
    one_face = sds((ny, nz))

    def stage(values_lo, values_hi, ends):
        lo_halo, hi_halo = jnp.where(on(X_ODD), *ends), jnp.where(on(X_ODD), *ends[::-1])
        lo_halo = jnp.where(on(X_LO), lo_halo, 0.0)
        hi_halo = jnp.where(on(X_HI), hi_halo, 0.0)
        to_lo = jnp.concatenate([lo_halo[:1], values_lo, hi_halo[:1]], axis=0)
        to_hi = jnp.concatenate([lo_halo[-1:], values_hi, hi_halo[-1:]], axis=0)
        return by_parity(Y_ODD, to_lo, to_hi)

    hx, hy, hz = nx // 2, ny // 2, nz // 2

    start, q, x_even, x_odd, *new = call(
        fine_start,
        (fine, fine) + (one_face,) * 4,
        in_specs=[SMEM] + [VMEM] * 2,
        out_specs=(VMEM,) * 6,
        flops=LONG,
    )(flags, rhs_fine, diag_fine)
    ends = exchange("group", x_even, x_odd)
    v, v_faces, q_faces, w_faces = call(
        fine_first,
        (fine, faces, faces, sds((4, 9, ny, nz), coup_fine.dtype)),
        in_specs=[VMEM] * 3,
        out_specs=(VMEM,) * 4,
        scratch_shapes=scratch + [pltpu.VMEM((2, 9, nx, nz), F32)],
        **heavy,
    )(start, q, coup_fine)
    ends, new, v_faces = lax.optimization_barrier((ends, new, v_faces))
    messages = stage(new[0], new[1], ends)
    messages, early_d = lax.optimization_barrier((messages, diag_mid))
    halo = ends + exchange("dev", *messages)
    slabs = sds((52 + WIDE, hy, hz))
    wx = call(
        mid_pack, (slabs, slabs), in_specs=[SMEM] + [VMEM] * 2, out_specs=(VMEM,) * 2
    )(flags, coup_mid, early_d)
    wx = exchange("group", *wx)
    halo, wx = lax.optimization_barrier((halo, wx))
    fix = call(
        fine_halo,
        (one_face,) * 6,
        in_specs=[SMEM] + [VMEM] * 7,
        out_specs=(VMEM,) * 6,
    )
    *new, x_even, x_odd = fix(flags, *halo, w_faces, v_faces, q_faces)

    ends = exchange("group", x_even, x_odd)
    v, v_faces = call(
        fine_next,
        (fine, faces),
        in_specs=[VMEM] * 8,
        out_specs=(VMEM,) * 2,
        scratch_shapes=scratch,
        **heavy,
    )(v, *new, start, q, coup_fine)
    ends, v_faces, new = lax.optimization_barrier((ends, v_faces, new))
    messages = stage(new[2], new[3], ends)
    messages, wx = lax.optimization_barrier((messages, wx))
    halo = ends + exchange("dev", *messages)
    w_wide, q_wide = call(
        mid_assemble,
        (sds((26, hx + 4, hy, hz), coup_mid.dtype), sds((hx + 2 * WIDE, hy, hz))),
        in_specs=[SMEM] + [VMEM] * 4,
        out_specs=(VMEM,) * 2,
    )(flags, coup_mid, diag_mid, *wx)
    halo, q_wide = lax.optimization_barrier((halo, q_wide))
    *new, x_even, x_odd = fix(flags, *halo, w_faces, v_faces, q_faces)

    ends = exchange("group", x_even, x_odd)
    fine_iterate, g_mid = call(
        fine_last,
        (fine, sds((hx, hy, hz))),
        in_specs=[VMEM] * 8,
        out_specs=(VMEM,) * 2,
        scratch_shapes=scratch + [pltpu.VMEM((hx * ny, nz), F32)],
        **heavy,
    )(v, *new, start, q, coup_fine)
    ends, g_mid, new = lax.optimization_barrier((ends, g_mid, new))
    halo = ends + exchange("dev", *stage(new[2], new[3], ends))
    f_mid, fx_even, fx_odd = call(
        fine_halo_last,
        (sds((hx, hy, hz)), sds((WIDE, hy, hz)), sds((WIDE, hy, hz))),
        in_specs=[SMEM] + [VMEM] * 6,
        out_specs=(VMEM,) * 3,
        scratch_shapes=[pltpu.VMEM((4 * ny, nz), F32)],
    )(flags, *halo, w_faces, g_mid)

    ex = hx + 2 * WIDE
    fx = exchange("group", fx_even, fx_odd)
    wide = sds((ex, hy, hz))
    mid_scratch = [pltpu.VMEM((9, ex, hy, hz), F32)]
    start_wide, *halo = call(
        mid_start,
        (wide, sds((ex, hz)), sds((ex, hz))),
        in_specs=[SMEM] + [VMEM] * 4,
        out_specs=(VMEM,) * 3,
    )(flags, f_mid, *fx, q_wide)
    v_mid = start_wide
    for reach in (WIDE, WIDE - 1):
        halo = exchange("dev", *halo)
        count = hx + 2 * reach - 2
        v_mid, *halo = call(
            functools.partial(mid_next, reach),
            (sds((count, hy, hz)), sds((count, hz)), sds((count, hz))),
            in_specs=[SMEM] + [VMEM] * 6,
            out_specs=(VMEM,) * 3,
            scratch_shapes=mid_scratch,
        )(flags, v_mid, *halo, start_wide, q_wide, w_wide)
    halo = exchange("dev", *halo)
    qx, qy, qz = hx // 2, hy // 2, hz // 2
    mid_iterate, source, outgoing = call(
        mid_last,
        (sds((hx, hy, hz)), sds((qx * qy, qz)), sds((slots, cells))),
        in_specs=[SMEM] * 2 + [VMEM] * 6,
        out_specs=(VMEM,) * 3,
        scratch_shapes=mid_scratch + [pltpu.VMEM((qx * hy, hz), F32)],
    )(flags, places, v_mid, *halo, f_mid, diag_mid, w_wide)

    arrived = lax.all_to_all(outgoing, "dev", split_axis=0, concat_axis=0, tiled=True)
    owned = call(solve_blocks, sds((slots, cells)), in_specs=[VMEM] * 2, out_specs=VMEM)(
        inverse_blocks.reshape(slots, cells, cells), arrived
    )
    returned = lax.all_to_all(owned, "dev", split_axis=0, concat_axis=0, tiled=True)
    correction, residual = call(
        finish,
        (sds((qx, qy, qz)), sds((qx, qy, qz))),
        in_specs=[SMEM] + [VMEM] * 4,
        out_specs=(VMEM,) * 2,
        scratch_shapes=[pltpu.VMEM((owners.shape[0], cells), F32)],
    )(
        places,
        returned,
        source,
        diag_coarse.reshape(qx * qy, qz),
        coup_coarse.reshape(26, qx * qy, qz),
    )
    return fine_iterate, mid_iterate, correction, residual


def solution(mesh):
    return jax.shard_map(
        shards,
        mesh=mesh,
        in_specs=(
            P("group", "dev", None),
            P("group", "dev", None),
            P(None, "group", "dev", None),
            P("group", "dev", None),
            P(None, "group", "dev", None),
            P("group", "dev", None),
            P(None, "group", "dev", None),
            P("group", "dev", None, None),
            P("group", "dev", None, None, None),
        ),
        out_specs=(
            P("group", "dev", None),
            P("group", "dev", None),
            P("group", "dev", None),
            P("group", "dev", None),
        ),
        check_vma=False,
    )
```

```python
import jax
import jax.numpy as jnp
from jax import lax
from jax.experimental import pallas as pl
from jax.experimental.pallas import tpu as pltpu
from jax.sharding import PartitionSpec as P

OMEGA = 0.8
HALVING = 0.5
OFFSETS = [
    (a, b, c)
    for a in (-1, 0, 1)
    for b in (-1, 0, 1)
    for c in (-1, 0, 1)
    if (a, b, c) != (0, 0, 0)
]
TO_YLO = [OFFSETS.index((a, -1, c)) for a in (-1, 0, 1) for c in (-1, 0, 1)]
TO_YHI = [OFFSETS.index((a, 1, c)) for a in (-1, 0, 1) for c in (-1, 0, 1)]
F32 = jnp.float32
VMEM_LIMIT = 20 * 1024 * 1024
XB = 4
WIDE = 3
SLABS = 52 + WIDE
X_LO, X_HI, Y_LO, Y_HI, X_ODD, Y_ODD = range(6)
LONG = 30_000_000_000
VMEM = pl.BlockSpec(memory_space=pltpu.VMEM)
SMEM = pl.BlockSpec(memory_space=pltpu.SMEM)


def sds(shape, dtype=F32):
    return jax.ShapeDtypeStruct(shape, dtype)


def iota(shape, dim):
    return lax.broadcasted_iota(jnp.int32, shape, dim)


def shift_z(v, c):
    if c == 0:
        return v
    n, dim = v.shape[-1], v.ndim - 1
    edge = 0 if c < 0 else n - 1
    return jnp.where(iota(v.shape, dim) == edge, 0.0, pltpu.roll(v, (-c) % n, dim))


def shift_y(v, b):
    if b == 0:
        return v
    n, dim = v.shape[-2], v.ndim - 2
    edge = 0 if b < 0 else n - 1
    return jnp.where(iota(v.shape, dim) == edge, 0.0, pltpu.roll(v, (-b) % n, dim))


def pair_sum_right(n, scale):
    return jnp.where((iota((n, n // 2), 0) >> 1) == iota((n, n // 2), 1), scale, 0.0).astype(F32)


def pair_sum_left(n):
    return jnp.where((iota((n // 2, n), 1) >> 1) == iota((n // 2, n), 0), 1.0, 0.0).astype(F32)


def parts_of(v):
    first = v.astype(jnp.bfloat16)
    rest = v - first.astype(F32)
    second = rest.astype(jnp.bfloat16)
    return first, second, (rest - second.astype(F32)).astype(jnp.bfloat16)


def dot_right(v, m):
    m = m.astype(jnp.bfloat16)
    return sum(jnp.dot(part, m, preferred_element_type=F32) for part in parts_of(v)[::-1])


def dot_left(m, v):
    m = m.astype(jnp.bfloat16)
    return sum(jnp.dot(m, part, preferred_element_type=F32) for part in parts_of(v)[::-1])


def put_versions(s_ref, x, layer):
    for c in (-1, 0, 1):
        along = shift_z(layer, c)
        for b in (-1, 0, 1):
            s_ref[(b + 1) * 3 + c + 1, x + 1] = shift_y(along, b)


def neighbours(w_ref, s_ref, first, at):
    total = [None] * XB
    for b in (-1, 0, 1):
        for c in (-1, 0, 1):
            k = (b + 1) * 3 + c + 1
            layers = [s_ref[k, first + r, :, at] for r in range(XB + 2)]
            for a in (-1, 0, 1):
                if (a, b, c) == (0, 0, 0):
                    continue
                o = OFFSETS.index((a, b, c))
                for i in range(XB):
                    term = w_ref[o, first + i, :, at].astype(F32) * layers[i + 1 + a]
                    total[i] = term if total[i] is None else total[i] + term
    return total


def lane_chunks(n):
    return [slice(k, k + 128) for k in range(0, n, 128)]


def zero_rims(s_ref):
    for edge in (0, s_ref.shape[1] - 1):
        for k in range(9):
            s_ref[k, edge] = jnp.zeros(s_ref.shape[2:], F32)


def patched(v_ref, new, x, last):
    xlo, xhi, ylo, yhi = new
    layer = v_ref[x]
    row = iota(layer.shape, 0)
    layer = jnp.where(row == 0, ylo[pl.ds(x, 1), :], layer)
    layer = jnp.where(row == layer.shape[0] - 1, yhi[pl.ds(x, 1), :], layer)
    layer = jnp.where(x == 0, xlo[...], layer)
    return jnp.where(x == last, xhi[...], layer)


def put_faces(faces_ref, v_ref):
    nx, ny = v_ref.shape[:2]
    faces_ref[0] = v_ref[0]
    faces_ref[1] = v_ref[nx - 1]
    for x in range(nx):
        faces_ref[2, x : x + 1, :] = v_ref[x, 0:1, :]
        faces_ref[3, x : x + 1, :] = v_ref[x, ny - 1 : ny, :]


def put_next(v_ref, start_ref, q_ref, w_ref, s_ref, j):
    for at in lane_chunks(v_ref.shape[2]):
        for i, total in enumerate(neighbours(w_ref, s_ref, j * XB, at)):
            x = j * XB + i
            centre = (1.0 - OMEGA) * s_ref[4, x + 1, :, at]
            v_ref[x, :, at] = centre + start_ref[x, :, at] + q_ref[x, :, at] * total


def fine_start(f_ref, d_ref, start_ref, q_ref, ylo, yhi):
    nx, ny = f_ref.shape[:2]

    @pl.loop(0, nx)
    def _(x):
        q = OMEGA / d_ref[x]
        q_ref[x] = q
        start_ref[x] = q * f_ref[x]

    for x in range(nx):
        ylo[x : x + 1, :] = start_ref[x, 0:1, :]
        yhi[x : x + 1, :] = start_ref[x, ny - 1 : ny, :]


def fine_first(
    _, start_ref, q_ref, w_ref, v_ref, faces_ref, qfaces_ref, wfaces_ref, s_ref, wy_ref
):
    nx, ny = v_ref.shape[:2]
    zero_rims(s_ref)

    @pl.loop(0, nx)
    def _(x):
        put_versions(s_ref, x, start_ref[x])

    @pl.loop(0, nx // XB)
    def _(j):
        put_next(v_ref, start_ref, q_ref, w_ref, s_ref, j)
        for i in range(XB):
            x = j * XB + i
            for k in range(9):
                wy_ref[0, k, pl.ds(x, 1), :] = w_ref[TO_YLO[k], x].astype(F32)[0:1, :]
                wy_ref[1, k, pl.ds(x, 1), :] = w_ref[TO_YHI[k], x].astype(F32)[ny - 1 : ny, :]

    wfaces_ref[0] = w_ref[0:9, 0]
    wfaces_ref[1] = w_ref[17:26, nx - 1]
    for k in range(9):
        wfaces_ref[2, k] = wy_ref[0, k].astype(wfaces_ref.dtype)
        wfaces_ref[3, k] = wy_ref[1, k].astype(wfaces_ref.dtype)
    put_faces(faces_ref, v_ref)
    put_faces(qfaces_ref, q_ref)


def fine_next(v_ref, xlo, xhi, ylo, yhi, start_ref, q_ref, w_ref, out_ref, faces_ref, s_ref):
    nx = v_ref.shape[0]
    zero_rims(s_ref)

    @pl.loop(0, nx)
    def _(x):
        put_versions(s_ref, x, patched(v_ref, (xlo, xhi, ylo, yhi), x, nx - 1))

    @pl.loop(0, nx // XB)
    def _(j):
        put_next(out_ref, start_ref, q_ref, w_ref, s_ref, j)

    put_faces(faces_ref, out_ref)


def fine_last(v_ref, xlo, xhi, ylo, yhi, start_ref, q_ref, w_ref, out_ref, g_ref, s_ref, p_ref):
    nx, ny, nz = v_ref.shape
    zero_rims(s_ref)

    @pl.loop(0, nx)
    def _(x):
        layer = patched(v_ref, (xlo, xhi, ylo, yhi), x, nx - 1)
        out_ref[x] = layer
        put_versions(s_ref, x, layer)

    @pl.loop(0, nx // XB)
    def _(j):
        for at in lane_chunks(nz):
            total = neighbours(w_ref, s_ref, j * XB, at)
            for i in range(XB):
                x = j * XB + i
                own = start_ref[x, :, at] - OMEGA * s_ref[4, x + 1, :, at]
                total[i] = total[i] + own / q_ref[x, :, at]
            for i in range(0, XB, 2):
                row = pl.multiple_of((j * (XB // 2) + i // 2) * ny, ny)
                p_ref[pl.ds(row, ny), at] = total[i] + total[i + 1]

    rows = dot_left(pair_sum_left(nx // 2 * ny), p_ref[...])
    g_ref[...] = dot_right(rows, pair_sum_right(nz, HALVING)).reshape(g_ref.shape)


def sides(flags, even, odd, lo, hi, parity):
    at_odd = flags[parity] > 0
    below = jnp.where(at_odd, even, odd)
    above = jnp.where(at_odd, odd, even)
    return jnp.where(flags[lo] > 0, below, 0.0), jnp.where(flags[hi] > 0, above, 0.0)


def halo_terms(flags, x_even, x_odd, y_even, y_odd, w_ref):
    xs, ys = [], []
    n = x_even.shape[0]
    x_sides = sides(flags, x_even[...], x_odd[...], X_LO, X_HI, X_ODD)
    y_sides = sides(flags, y_even[...], y_odd[...], Y_LO, Y_HI, Y_ODD)
    for side, halo in enumerate(x_sides):
        total = None
        for c in (-1, 0, 1):
            along = shift_z(halo, c)
            for b in (-1, 0, 1):
                term = w_ref[side, (b + 1) * 3 + c + 1].astype(F32) * shift_y(along, b)
                total = term if total is None else total + term
        xs.append(total)
    for side, halo in enumerate(y_sides):
        total = None
        for c in (-1, 0, 1):
            along = shift_z(halo, c)
            for a in (-1, 0, 1):
                term = w_ref[2 + side, (a + 1) * 3 + c + 1].astype(F32) * along[1 + a : 1 + a + n]
                total = term if total is None else total + term
        ys.append(total)
    return xs, ys


def fine_halo(flags, x_even, x_odd, y_even, y_odd, w_ref, faces_ref, q_ref, *outs):
    xs, ys = halo_terms(flags, x_even, x_odd, y_even, y_odd, w_ref)
    n = xs[0].shape[0]
    row = iota(xs[0].shape, 0)

    def crossed(own, others, place):
        own = jnp.where(row == 0, own + others[0][place : place + 1], own)
        return jnp.where(row == n - 1, own + others[1][place : place + 1], own)

    sums = [
        crossed(xs[0], ys, 0),
        crossed(xs[1], ys, n - 1),
        crossed(ys[0], xs, 0),
        crossed(ys[1], xs, n - 1),
    ]
    new = [faces_ref[k] + q_ref[k] * sums[k] for k in range(4)]
    for k in range(4):
        outs[k][...] = new[k]
    at_odd = flags[X_ODD] > 0
    outs[4][...] = jnp.where(at_odd, new[0], new[1])
    outs[5][...] = jnp.where(at_odd, new[1], new[0])


def fine_halo_last(
    flags, x_even, x_odd, y_even, y_odd, w_ref, g_ref, f_ref, to_even, to_odd, t_ref
):
    xs, ys = halo_terms(flags, x_even, x_odd, y_even, y_odd, w_ref)
    n, nz = xs[0].shape
    for k, part in enumerate(xs + ys):
        t_ref[k * n : (k + 1) * n, :] = part
    rows = dot_left(pair_sum_left(4 * n), t_ref[...])
    half = n // 2
    coarse = dot_right(rows, pair_sum_right(nz, HALVING))
    row = iota((half, nz // 2), 0)
    for i in range(half):
        total = g_ref[i]
        total = total + jnp.where(row == 0, coarse[2 * half + i : 2 * half + i + 1], 0.0)
        total = total + jnp.where(row == half - 1, coarse[3 * half + i : 3 * half + i + 1], 0.0)
        if i == 0:
            total = total + coarse[0:half]
        if i == half - 1:
            total = total + coarse[half : 2 * half]
        f_ref[i] = total
    at_odd = flags[X_ODD] > 0
    for k in range(WIDE):
        lo, hi = f_ref[k], f_ref[half - WIDE + k]
        to_even[k] = jnp.where(at_odd, lo, hi)
        to_odd[k] = jnp.where(at_odd, hi, lo)


def put_both(at_odd, even_ref, odd_ref, index, lo, hi):
    even_ref[index] = jnp.where(at_odd, lo, hi)
    odd_ref[index] = jnp.where(at_odd, hi, lo)


def mid_pack(flags, w_ref, d_ref, x_even, x_odd):
    nx = d_ref.shape[0]
    at_odd = flags[X_ODD] > 0

    @pl.loop(0, 26)
    def _(o):
        for k in range(2):
            lo, hi = w_ref[o, k].astype(F32), w_ref[o, nx - 2 + k].astype(F32)
            put_both(at_odd, x_even, x_odd, o * 2 + k, lo, hi)

    for k in range(WIDE):
        put_both(at_odd, x_even, x_odd, 52 + k, d_ref[k], d_ref[nx - WIDE + k])


def layer_beyond(flags, even, odd, index, below):
    at_odd = flags[X_ODD] > 0
    first, second = (even, odd) if below else (odd, even)
    return jnp.where(at_odd, first[index], second[index])


def mid_pack_y(flags, w_ref, d_ref, x_even, x_odd, to_even, to_odd):
    nx, ny = d_ref.shape[:2]
    at_odd = flags[Y_ODD] > 0

    def put_row(place, r, lo, hi):
        put_both(at_odd, to_even, to_odd, (place, slice(r, r + 1), slice(None)), lo, hi)

    @pl.loop(0, 26)
    def _(o):
        for x in range(nx):
            layer = w_ref[o, x].astype(F32)
            for k in range(2):
                put_row(o * 2 + k, x, layer[k : k + 1], layer[ny - 2 + k : ny - 1 + k])

    for k in range(WIDE):
        for x in range(nx):
            r = ny - WIDE + k
            put_row(52 + k, x, d_ref[x, k : k + 1, :], d_ref[x, r : r + 1, :])

    @pl.loop(0, 26)
    def _(o):
        for e in range(4):
            layer = layer_beyond(flags, x_even, x_odd, o * 2 + e % 2, e < 2)
            for k in range(2):
                lo, hi = layer[k : k + 1], layer[ny - 2 + k : ny - 1 + k]
                put_row(SLABS + o, k * 4 + e, lo, hi)

    for e in range(2 * WIDE):
        layer = layer_beyond(flags, x_even, x_odd, 52 + e % WIDE, e < WIDE)
        for k in range(WIDE):
            r = ny - WIDE + k
            put_row(SLABS + 26 + k, e, layer[k : k + 1], layer[r : r + 1])


def mid_assemble(flags, w_ref, d_ref, x_even, x_odd, y_even, y_odd, w_out, d_out, t_ref):
    nx, ny, nz = d_ref.shape
    at_odd = flags[Y_ODD] > 0
    t_ref[...] = jnp.zeros(t_ref.shape, F32)

    def put(o, x, layer, place, r):
        t_ref[x + 2, 3 : 3 + ny, :] = layer
        for k in range(2):
            index = (place(k), slice(r(k), r(k) + 1), slice(None))
            even, odd = y_even[index], y_odd[index]
            t_ref[x + 2, 1 + k : 2 + k, :] = jnp.where(at_odd, even, odd)
            t_ref[x + 2, 3 + ny + k : 4 + ny + k, :] = jnp.where(at_odd, odd, even)
        w_out[o, x + 2] = t_ref[x + 2].astype(w_out.dtype)

    @pl.loop(0, 26)
    def _(o):
        for x in range(nx):
            put(o, x, w_ref[o, x].astype(F32), lambda k: o * 2 + k, lambda k: x)
        for e, x in enumerate((-2, -1, nx, nx + 1)):
            layer = layer_beyond(flags, x_even, x_odd, o * 2 + e % 2, e < 2)
            put(o, x, layer, lambda k: SLABS + o, lambda k: k * 4 + e)

    d_out[...] = jnp.ones(d_out.shape, F32)
    for x in range(-WIDE, nx + WIDE):
        r = x + WIDE
        if 0 <= x < nx:
            layer, place, e = d_ref[x], 52, x
        else:
            e = r if x < 0 else r - nx
            layer, place = layer_beyond(flags, x_even, x_odd, 52 + e % WIDE, x < 0), SLABS + 26
        d_out[r, 3 : 3 + ny, :] = layer
        for k in range(WIDE):
            even, odd = y_even[place + k, e : e + 1, :], y_odd[place + k, e : e + 1, :]
            d_out[r, k : k + 1, :] = jnp.where(at_odd, even, odd)
            d_out[r, 3 + ny + k : 4 + ny + k, :] = jnp.where(at_odd, odd, even)


def swap_blocks(values):
    n, lanes = values.shape
    width = lanes // n
    wide = jnp.broadcast_to(values[None], (n, n, lanes))
    wide = jnp.where(iota(wide.shape, 2) // width == iota(wide.shape, 0), wide, 0.0)
    spread = jnp.where(
        iota((lanes, lanes), 0) % width == iota((lanes, lanes), 1) % width, 1.0, 0.0
    ).astype(F32)
    moved = dot_right(wide.reshape(n * n, lanes), spread).reshape(n, n, lanes)
    moved = jnp.where(iota(moved.shape, 2) // width == iota(moved.shape, 1), moved, 0.0)
    return jnp.sum(moved, axis=1)


def mid_rounds(
    flags,
    places,
    fx_ref,
    fy_even,
    fy_odd,
    d_ref,
    w_ref,
    mid_out,
    src_out,
    slot_out,
    f_ref,
    v_ref,
    s_ref,
    p_ref,
):
    ex, ey, nz = f_ref.shape
    ny = fx_ref.shape[1]
    nx = ex - 2 * WIDE
    row = iota((ey, nz), 0)

    def inside(x, reach):
        lo = jnp.where(flags[Y_LO] > 0, WIDE - reach, WIDE)
        hi = jnp.where(flags[Y_HI] > 0, WIDE + ny + reach, WIDE + ny)
        ok = (row >= lo) & (row < hi)
        if x < 0:
            ok = ok & (flags[X_LO] > 0)
        if x >= nx:
            ok = ok & (flags[X_HI] > 0)
        return ok

    for r in range(ex):
        f_ref[r] = jnp.zeros((ey, nz), F32)
        f_ref[r, WIDE : WIDE + ny, :] = fx_ref[r]
        even, odd = fy_even[r], fy_odd[r]
        f_ref[r, 0:WIDE, :] = jnp.where(flags[Y_ODD] > 0, even, odd)
        f_ref[r, WIDE + ny : 2 * WIDE + ny, :] = jnp.where(flags[Y_ODD] > 0, odd, even)
        v_ref[r] = jnp.where(inside(r - WIDE, WIDE), OMEGA * f_ref[r] / d_ref[r], 0.0)

    def spread(reach):
        for r in range(WIDE - reach, WIDE + nx + reach):
            layer = v_ref[r]
            for c in (-1, 0, 1):
                along = shift_z(layer, c)
                for b in (-1, 0, 1):
                    s_ref[(b + 1) * 3 + c + 1, r] = shift_y(along, b)

    def leftover(r):
        total = f_ref[r] - d_ref[r] * v_ref[r]
        for o, (a, b, c) in enumerate(OFFSETS):
            total = total + w_ref[o, r - 1].astype(F32) * s_ref[(b + 1) * 3 + c + 1, r + a]
        return total

    for reach in (2, 1):
        spread(reach + 1)
        for r in range(WIDE - reach, WIDE + nx + reach):
            new = v_ref[r] + OMEGA * leftover(r) / d_ref[r]
            v_ref[r] = jnp.where(inside(r - WIDE, reach), new, 0.0)
    for x in range(nx):
        mid_out[x] = v_ref[WIDE + x][WIDE : WIDE + ny]
    spread(1)
    for i in range(nx // 2):
        r = WIDE + 2 * i
        p_ref[i * ey : (i + 1) * ey, :] = leftover(r) + leftover(r + 1)

    half = ny // 2
    rows = nx // 2 * half
    out_row = iota((rows, nx // 2 * ey), 0)
    in_row = iota((rows, nx // 2 * ey), 1)
    first = (out_row // half) * ey + WIDE + 2 * (out_row % half)
    left_sum = jnp.where((in_row == first) | (in_row == first + 1), 1.0, 0.0).astype(F32)
    source = dot_right(dot_left(left_sum, p_ref[...]), pair_sum_right(nz, HALVING))
    src_out[...] = source
    blocked = swap_blocks(source)
    slot_out[...] = jnp.zeros(slot_out.shape, F32)
    for k in range(blocked.shape[0]):
        slot_out[pl.ds(places[k], 1), :] = blocked[k : k + 1]


def solve_blocks(m_ref, a_ref, out_ref):
    slots, cells = a_ref.shape
    lane = iota((cells, cells), 1)
    columns = jnp.zeros((cells, cells), F32)
    for q in range(slots):
        product = jnp.sum(m_ref[q] * a_ref[q : q + 1, :], axis=1, keepdims=True)
        columns = jnp.where(lane == q, product, columns)
    out_ref[...] = columns.T[0:slots]


def finish(places, back_ref, src_ref, dc_ref, wc_ref, cor_out, res_out, c_ref):
    blocks, cells = c_ref.shape
    nx, half = cor_out.shape[:2]
    rows = nx * half
    for k in range(blocks):
        c_ref[k : k + 1, :] = back_ref[pl.ds(places[k], 1), :]
    correction = swap_blocks(c_ref[...])
    source = src_ref[...]
    grid_row = iota(source.shape, 0)
    width = cells // blocks
    zpos = iota(source.shape, 1) % width
    residual = source - dc_ref[...] * correction
    for o, (a, b, c) in enumerate(OFFSETS):
        moved = correction
        if c:
            moved = pltpu.roll(moved, (-c) % cells, 1)
            moved = jnp.where(zpos == (0 if c < 0 else width - 1), 0.0, moved)
        if a or b:
            moved = pltpu.roll(moved, (-(a * half + b)) % rows, 0)
            y, x = grid_row % half + b, grid_row // half + a
            ok = (y >= 0) & (y < half) & (x >= 0) & (x < nx)
            moved = jnp.where(ok, moved, 0.0)
        residual = residual + wc_ref[o].astype(F32) * moved
    for x in range(nx):
        cor_out[x] = correction[x * half : (x + 1) * half]
        res_out[x] = residual[x * half : (x + 1) * half]


def block_ranks(owners):
    same = owners[:, None] == owners[None, :]
    count = owners.shape[0]
    earlier = jnp.arange(count)[None, :] < jnp.arange(count)[:, None]
    return jnp.sum((same & earlier).astype(jnp.int32), axis=-1)


def call(body, outs, ins=None, **more):
    flops = more.pop("flops", 1_000_000)
    size = more.pop("size", 1_000_000)
    limit = more.pop("limit", VMEM_LIMIT)
    return pl.pallas_call(
        body,
        out_shape=outs,
        cost_estimate=pl.CostEstimate(flops=flops, bytes_accessed=size, transcendentals=0),
        compiler_params=pltpu.CompilerParams(vmem_limit_bytes=limit),
        **more,
    )


def pairs(axis):
    size = lax.axis_size(axis)
    even = [(i, i ^ 1) for i in range(size)]
    odd = [(i, (i + 1) % size if i % 2 else (i - 1) % size) for i in range(size)]
    return even, odd


def exchange(axis, to_even, to_odd):
    even, odd = pairs(axis)
    return lax.ppermute(to_even, axis, even), lax.ppermute(to_odd, axis, odd)


def shards(
    rhs_fine,
    diag_fine,
    coup_fine,
    diag_mid,
    coup_mid,
    diag_coarse,
    coup_coarse,
    owner_map,
    inverse_blocks,
):
    nx, ny, nz = rhs_fine.shape
    g, d = lax.axis_index("group"), lax.axis_index("dev")
    n_group, n_dev = lax.axis_size("group"), lax.axis_size("dev")
    flags = jnp.stack([g > 0, g < n_group - 1, d > 0, d < n_dev - 1, g % 2 > 0, d % 2 > 0])
    slots, cells = inverse_blocks.shape[2], inverse_blocks.shape[3]
    owners = owner_map.reshape(-1)
    places = owners * (slots // n_dev) + block_ranks(owners)
    flags = flags.astype(jnp.int32)
    masks = jnp.broadcast_to(flags.astype(F32)[:, None], (6, rhs_fine.shape[2]))
    flags, masks = lax.optimization_barrier((flags, masks))

    def on(place, width=nz):
        return masks[place : place + 1, :width] > 0.5

    def by_parity(parity, lo, hi):
        at_odd = on(parity, lo.shape[-1])
        return jnp.where(at_odd, lo, hi), jnp.where(at_odd, hi, lo)

    scratch = [pltpu.VMEM((9, nx + 2, ny, nz), F32)]
    fine = sds((nx, ny, nz))
    faces = sds((4, ny, nz))
    heavy = dict(flops=60 * nx * ny * nz, size=coup_fine.size * 2 + 4 * rhs_fine.size * 4)
    one_face = sds((ny, nz))

    def stage(values_lo, values_hi, ends):
        lo_halo, hi_halo = jnp.where(on(X_ODD), *ends), jnp.where(on(X_ODD), *ends[::-1])
        lo_halo = jnp.where(on(X_LO), lo_halo, 0.0)
        hi_halo = jnp.where(on(X_HI), hi_halo, 0.0)
        to_lo = jnp.concatenate([lo_halo[:1], values_lo, hi_halo[:1]], axis=0)
        to_hi = jnp.concatenate([lo_halo[-1:], values_hi, hi_halo[-1:]], axis=0)
        return by_parity(Y_ODD, to_lo, to_hi)

    hx, hy, hz = nx // 2, ny // 2, nz // 2

    faces_now = [OMEGA / diag_fine[x] * rhs_fine[x] for x in (0, nx - 1)]
    ends = exchange("group", *by_parity(X_ODD, *faces_now))
    start, q, *new = call(
        fine_start,
        (fine, fine) + (one_face,) * 2,
        in_specs=[VMEM] * 2,
        out_specs=(VMEM,) * 4,
        flops=LONG,
    )(rhs_fine, diag_fine)
    ends, new = lax.optimization_barrier((ends, new))
    messages = stage(new[0], new[1], ends)
    messages, late = lax.optimization_barrier((messages, flags))
    v, v_faces, q_faces, w_faces = call(
        fine_first,
        (fine, faces, faces, sds((4, 9, ny, nz), coup_fine.dtype)),
        in_specs=[SMEM] + [VMEM] * 3,
        out_specs=(VMEM,) * 4,
        scratch_shapes=scratch + [pltpu.VMEM((2, 9, nx, nz), F32)],
        **heavy,
    )(late, start, q, coup_fine)
    halo = ends + exchange("dev", *messages)
    fix = call(
        fine_halo,
        (one_face,) * 6,
        in_specs=[SMEM] + [VMEM] * 7,
        out_specs=(VMEM,) * 6,
    )
    *new, x_even, x_odd = fix(flags, *halo, w_faces, v_faces, q_faces)

    ends = exchange("group", x_even, x_odd)
    v, v_faces = call(
        fine_next,
        (fine, faces),
        in_specs=[VMEM] * 8,
        out_specs=(VMEM,) * 2,
        scratch_shapes=scratch,
        **heavy,
    )(v, *new, start, q, coup_fine)
    ends, v_faces, new = lax.optimization_barrier((ends, v_faces, new))
    messages = stage(new[2], new[3], ends)
    messages, late = lax.optimization_barrier((messages, flags))
    halo = ends + exchange("dev", *messages)
    slabs = sds((SLABS, hy, hz))
    wx = call(
        mid_pack,
        (slabs, slabs),
        in_specs=[SMEM] + [VMEM] * 2,
        out_specs=(VMEM,) * 2,
        flops=LONG,
    )(late, coup_mid, diag_mid)
    wx = exchange("group", *wx)
    *new, x_even, x_odd = fix(flags, *halo, w_faces, v_faces, q_faces)

    ends = exchange("group", x_even, x_odd)
    fine_iterate, g_mid = call(
        fine_last,
        (fine, sds((hx, hy, hz))),
        in_specs=[VMEM] * 8,
        out_specs=(VMEM,) * 2,
        scratch_shapes=scratch + [pltpu.VMEM((hx * ny, nz), F32)],
        **heavy,
    )(v, *new, start, q, coup_fine)
    ends, g_mid, new, wx = lax.optimization_barrier((ends, g_mid, new, wx))
    messages = stage(new[2], new[3], ends)
    messages, late = lax.optimization_barrier((messages, flags))
    halo = ends + exchange("dev", *messages)
    strips = sds((SLABS + 26 + WIDE, hx, hz))
    wy = call(
        mid_pack_y,
        (strips, strips),
        in_specs=[SMEM] + [VMEM] * 4,
        out_specs=(VMEM,) * 2,
        flops=LONG,
    )(late, coup_mid, diag_mid, *wx)
    halo, wy = lax.optimization_barrier((halo, wy))
    wy = exchange("dev", *wy)
    f_mid, fx_even, fx_odd = call(
        fine_halo_last,
        (sds((hx, hy, hz)), sds((WIDE, hy, hz)), sds((WIDE, hy, hz))),
        in_specs=[SMEM] + [VMEM] * 6,
        out_specs=(VMEM,) * 3,
        scratch_shapes=[pltpu.VMEM((4 * ny, nz), F32)],
    )(flags, *halo, w_faces, g_mid)

    fx_even, fx_odd = exchange("group", fx_even, fx_odd)
    fx_even, fx_odd, wy = lax.optimization_barrier((fx_even, fx_odd, wy))
    at_odd = on(X_ODD, hz)
    fx_lo, fx_hi = jnp.where(at_odd, fx_even, fx_odd), jnp.where(at_odd, fx_odd, fx_even)
    fx = jnp.concatenate([fx_lo, f_mid, fx_hi], axis=0)
    fy = exchange("dev", *by_parity(Y_ODD, fx[:, :WIDE], fx[:, hy - WIDE :]))
    ex, ey = hx + 2 * WIDE, 16
    w_wide, d_wide = call(
        mid_assemble,
        (sds((26, hx + 4, ey, hz), coup_mid.dtype), sds((ex, ey, hz))),
        in_specs=[SMEM] + [VMEM] * 6,
        out_specs=(VMEM,) * 2,
        scratch_shapes=[pltpu.VMEM((hx + 4, ey, hz), F32)],
    )(flags, coup_mid, diag_mid, *wx, *wy)
    qx, qy, qz = hx // 2, hy // 2, hz // 2
    mid_iterate, source, outgoing = call(
        mid_rounds,
        (sds((hx, hy, hz)), sds((qx * qy, qz)), sds((slots, cells))),
        in_specs=[SMEM] * 2 + [VMEM] * 5,
        out_specs=(VMEM,) * 3,
        scratch_shapes=[
            pltpu.VMEM((ex, ey, hz), F32),
            pltpu.VMEM((ex, ey, hz), F32),
            pltpu.VMEM((9, ex, ey, hz), F32),
            pltpu.VMEM((hx // 2 * ey, hz), F32),
        ],
        flops=20_000_000,
    )(flags, places, fx, *fy, d_wide, w_wide)

    arrived = lax.all_to_all(outgoing, "dev", split_axis=0, concat_axis=0, tiled=True)
    owned = call(solve_blocks, sds((slots, cells)), in_specs=[VMEM] * 2, out_specs=VMEM)(
        inverse_blocks.reshape(slots, cells, cells), arrived
    )
    returned = lax.all_to_all(owned, "dev", split_axis=0, concat_axis=0, tiled=True)
    correction, residual = call(
        finish,
        (sds((qx, qy, qz)), sds((qx, qy, qz))),
        in_specs=[SMEM] + [VMEM] * 4,
        out_specs=(VMEM,) * 2,
        scratch_shapes=[pltpu.VMEM((owners.shape[0], cells), F32)],
    )(
        places,
        returned,
        source,
        diag_coarse.reshape(qx * qy, qz),
        coup_coarse.reshape(26, qx * qy, qz),
    )
    return fine_iterate, mid_iterate, correction, residual


def solution(mesh):
    return jax.shard_map(
        shards,
        mesh=mesh,
        in_specs=(
            P("group", "dev", None),
            P("group", "dev", None),
            P(None, "group", "dev", None),
            P("group", "dev", None),
            P(None, "group", "dev", None),
            P("group", "dev", None),
            P(None, "group", "dev", None),
            P("group", "dev", None, None),
            P("group", "dev", None, None, None),
        ),
        out_specs=(
            P("group", "dev", None),
            P("group", "dev", None),
            P("group", "dev", None),
            P("group", "dev", None),
        ),
        check_vma=False,
    )
```

```python
import jax
import jax.numpy as jnp
from jax import lax
from jax.experimental import pallas as pl
from jax.experimental.pallas import tpu as pltpu
from jax.sharding import PartitionSpec as P

OMEGA = 0.8
HALVING = 0.5
OFFSETS = [
    (a, b, c)
    for a in (-1, 0, 1)
    for b in (-1, 0, 1)
    for c in (-1, 0, 1)
    if (a, b, c) != (0, 0, 0)
]
TO_YLO = [OFFSETS.index((a, -1, c)) for a in (-1, 0, 1) for c in (-1, 0, 1)]
TO_YHI = [OFFSETS.index((a, 1, c)) for a in (-1, 0, 1) for c in (-1, 0, 1)]
F32 = jnp.float32
VMEM_LIMIT = 20 * 1024 * 1024
XB = 4
WIDE = 3
SLABS = 52 + WIDE
X_LO, X_HI, Y_LO, Y_HI, X_ODD, Y_ODD = range(6)
LONG = 30_000_000_000
VMEM = pl.BlockSpec(memory_space=pltpu.VMEM)
SMEM = pl.BlockSpec(memory_space=pltpu.SMEM)


def sds(shape, dtype=F32):
    return jax.ShapeDtypeStruct(shape, dtype)


def iota(shape, dim):
    return lax.broadcasted_iota(jnp.int32, shape, dim)


def shift_z(v, c):
    if c == 0:
        return v
    n, dim = v.shape[-1], v.ndim - 1
    edge = 0 if c < 0 else n - 1
    return jnp.where(iota(v.shape, dim) == edge, 0.0, pltpu.roll(v, (-c) % n, dim))


def shift_y(v, b):
    if b == 0:
        return v
    n, dim = v.shape[-2], v.ndim - 2
    edge = 0 if b < 0 else n - 1
    return jnp.where(iota(v.shape, dim) == edge, 0.0, pltpu.roll(v, (-b) % n, dim))


def pair_sum_right(n, scale):
    return jnp.where((iota((n, n // 2), 0) >> 1) == iota((n, n // 2), 1), scale, 0.0).astype(F32)


def pair_sum_left(n):
    return jnp.where((iota((n // 2, n), 1) >> 1) == iota((n // 2, n), 0), 1.0, 0.0).astype(F32)


def parts_of(v):
    first = v.astype(jnp.bfloat16)
    rest = v - first.astype(F32)
    second = rest.astype(jnp.bfloat16)
    return first, second, (rest - second.astype(F32)).astype(jnp.bfloat16)


def dot_right(v, m):
    m = m.astype(jnp.bfloat16)
    return sum(jnp.dot(part, m, preferred_element_type=F32) for part in parts_of(v)[::-1])


def dot_left(m, v):
    m = m.astype(jnp.bfloat16)
    return sum(jnp.dot(m, part, preferred_element_type=F32) for part in parts_of(v)[::-1])


def put_versions(s_ref, x, layer):
    for c in (-1, 0, 1):
        along = shift_z(layer, c)
        for b in (-1, 0, 1):
            s_ref[(b + 1) * 3 + c + 1, x + 1] = shift_y(along, b)


def neighbours(w_ref, s_ref, first, at):
    total = [None] * XB
    for b in (-1, 0, 1):
        for c in (-1, 0, 1):
            k = (b + 1) * 3 + c + 1
            layers = [s_ref[k, first + r, :, at] for r in range(XB + 2)]
            for a in (-1, 0, 1):
                if (a, b, c) == (0, 0, 0):
                    continue
                o = OFFSETS.index((a, b, c))
                for i in range(XB):
                    term = w_ref[o, first + i, :, at].astype(F32) * layers[i + 1 + a]
                    total[i] = term if total[i] is None else total[i] + term
    return total


def lane_chunks(n):
    return [slice(k, k + 128) for k in range(0, n, 128)]


def zero_rims(s_ref):
    for edge in (0, s_ref.shape[1] - 1):
        for k in range(9):
            s_ref[k, edge] = jnp.zeros(s_ref.shape[2:], F32)


def patched(v_ref, new, x, last):
    xlo, xhi, ylo, yhi = new
    layer = v_ref[x]
    row = iota(layer.shape, 0)
    layer = jnp.where(row == 0, ylo[pl.ds(x, 1), :], layer)
    layer = jnp.where(row == layer.shape[0] - 1, yhi[pl.ds(x, 1), :], layer)
    layer = jnp.where(x == 0, xlo[...], layer)
    return jnp.where(x == last, xhi[...], layer)


def put_faces(faces_ref, v_ref):
    nx, ny = v_ref.shape[:2]
    faces_ref[0] = v_ref[0]
    faces_ref[1] = v_ref[nx - 1]
    for x in range(nx):
        faces_ref[2, x : x + 1, :] = v_ref[x, 0:1, :]
        faces_ref[3, x : x + 1, :] = v_ref[x, ny - 1 : ny, :]


def put_next(v_ref, start_ref, q_ref, w_ref, s_ref, j):
    for at in lane_chunks(v_ref.shape[2]):
        for i, total in enumerate(neighbours(w_ref, s_ref, j * XB, at)):
            x = j * XB + i
            centre = (1.0 - OMEGA) * s_ref[4, x + 1, :, at]
            v_ref[x, :, at] = centre + start_ref[x, :, at] + q_ref[x, :, at] * total


def fine_start(f_ref, d_ref, start_ref, q_ref, ylo, yhi):
    nx, ny = f_ref.shape[:2]

    @pl.loop(0, nx)
    def _(x):
        q = OMEGA / d_ref[x]
        q_ref[x] = q
        start_ref[x] = q * f_ref[x]

    for x in range(nx):
        ylo[x : x + 1, :] = start_ref[x, 0:1, :]
        yhi[x : x + 1, :] = start_ref[x, ny - 1 : ny, :]


def fine_first(
    _, start_ref, q_ref, w_ref, v_ref, faces_ref, qfaces_ref, wfaces_ref, s_ref, wy_ref
):
    nx, ny = v_ref.shape[:2]
    zero_rims(s_ref)

    @pl.loop(0, nx)
    def _(x):
        put_versions(s_ref, x, start_ref[x])

    @pl.loop(0, nx // XB)
    def _(j):
        put_next(v_ref, start_ref, q_ref, w_ref, s_ref, j)
        for i in range(XB):
            x = j * XB + i
            for k in range(9):
                wy_ref[0, k, pl.ds(x, 1), :] = w_ref[TO_YLO[k], x].astype(F32)[0:1, :]
                wy_ref[1, k, pl.ds(x, 1), :] = w_ref[TO_YHI[k], x].astype(F32)[ny - 1 : ny, :]

    wfaces_ref[0] = w_ref[0:9, 0]
    wfaces_ref[1] = w_ref[17:26, nx - 1]
    for k in range(9):
        wfaces_ref[2, k] = wy_ref[0, k].astype(wfaces_ref.dtype)
        wfaces_ref[3, k] = wy_ref[1, k].astype(wfaces_ref.dtype)
    put_faces(faces_ref, v_ref)
    put_faces(qfaces_ref, q_ref)


def fine_next(v_ref, xlo, xhi, ylo, yhi, start_ref, q_ref, w_ref, out_ref, faces_ref, s_ref):
    nx = v_ref.shape[0]
    zero_rims(s_ref)

    @pl.loop(0, nx)
    def _(x):
        put_versions(s_ref, x, patched(v_ref, (xlo, xhi, ylo, yhi), x, nx - 1))

    @pl.loop(0, nx // XB)
    def _(j):
        put_next(out_ref, start_ref, q_ref, w_ref, s_ref, j)

    put_faces(faces_ref, out_ref)


def fine_last(v_ref, xlo, xhi, ylo, yhi, start_ref, q_ref, w_ref, out_ref, g_ref, s_ref, p_ref):
    nx, ny, nz = v_ref.shape
    zero_rims(s_ref)

    @pl.loop(0, nx)
    def _(x):
        layer = patched(v_ref, (xlo, xhi, ylo, yhi), x, nx - 1)
        out_ref[x] = layer
        put_versions(s_ref, x, layer)

    @pl.loop(0, nx // XB)
    def _(j):
        for at in lane_chunks(nz):
            total = neighbours(w_ref, s_ref, j * XB, at)
            for i in range(XB):
                x = j * XB + i
                own = start_ref[x, :, at] - OMEGA * s_ref[4, x + 1, :, at]
                total[i] = total[i] + own / q_ref[x, :, at]
            for i in range(0, XB, 2):
                row = pl.multiple_of((j * (XB // 2) + i // 2) * ny, ny)
                p_ref[pl.ds(row, ny), at] = total[i] + total[i + 1]

    rows = dot_left(pair_sum_left(nx // 2 * ny), p_ref[...])
    g_ref[...] = dot_right(rows, pair_sum_right(nz, HALVING)).reshape(g_ref.shape)


def sides(flags, even, odd, lo, hi, parity):
    at_odd = flags[parity] > 0
    below = jnp.where(at_odd, even, odd)
    above = jnp.where(at_odd, odd, even)
    return jnp.where(flags[lo] > 0, below, 0.0), jnp.where(flags[hi] > 0, above, 0.0)


def halo_terms(flags, x_even, x_odd, y_even, y_odd, w_ref):
    xs, ys = [], []
    n = x_even.shape[0]
    x_sides = sides(flags, x_even[...], x_odd[...], X_LO, X_HI, X_ODD)
    y_sides = sides(flags, y_even[...], y_odd[...], Y_LO, Y_HI, Y_ODD)
    for side, halo in enumerate(x_sides):
        total = None
        for c in (-1, 0, 1):
            along = shift_z(halo, c)
            for b in (-1, 0, 1):
                term = w_ref[side, (b + 1) * 3 + c + 1].astype(F32) * shift_y(along, b)
                total = term if total is None else total + term
        xs.append(total)
    for side, halo in enumerate(y_sides):
        total = None
        for c in (-1, 0, 1):
            along = shift_z(halo, c)
            for a in (-1, 0, 1):
                term = w_ref[2 + side, (a + 1) * 3 + c + 1].astype(F32) * along[1 + a : 1 + a + n]
                total = term if total is None else total + term
        ys.append(total)
    return xs, ys


def fine_halo(flags, x_even, x_odd, y_even, y_odd, w_ref, faces_ref, q_ref, *outs):
    xs, ys = halo_terms(flags, x_even, x_odd, y_even, y_odd, w_ref)
    n = xs[0].shape[0]
    row = iota(xs[0].shape, 0)

    def crossed(own, others, place):
        own = jnp.where(row == 0, own + others[0][place : place + 1], own)
        return jnp.where(row == n - 1, own + others[1][place : place + 1], own)

    sums = [
        crossed(xs[0], ys, 0),
        crossed(xs[1], ys, n - 1),
        crossed(ys[0], xs, 0),
        crossed(ys[1], xs, n - 1),
    ]
    new = [faces_ref[k] + q_ref[k] * sums[k] for k in range(4)]
    for k in range(4):
        outs[k][...] = new[k]
    at_odd = flags[X_ODD] > 0
    outs[4][...] = jnp.where(at_odd, new[0], new[1])
    outs[5][...] = jnp.where(at_odd, new[1], new[0])


def fine_halo_last(
    flags, x_even, x_odd, y_even, y_odd, w_ref, g_ref, f_ref, to_even, to_odd, t_ref
):
    xs, ys = halo_terms(flags, x_even, x_odd, y_even, y_odd, w_ref)
    n, nz = xs[0].shape
    for k, part in enumerate(xs + ys):
        t_ref[k * n : (k + 1) * n, :] = part
    rows = dot_left(pair_sum_left(4 * n), t_ref[...])
    half = n // 2
    coarse = dot_right(rows, pair_sum_right(nz, HALVING))
    row = iota((half, nz // 2), 0)
    for i in range(half):
        total = g_ref[i]
        total = total + jnp.where(row == 0, coarse[2 * half + i : 2 * half + i + 1], 0.0)
        total = total + jnp.where(row == half - 1, coarse[3 * half + i : 3 * half + i + 1], 0.0)
        if i == 0:
            total = total + coarse[0:half]
        if i == half - 1:
            total = total + coarse[half : 2 * half]
        f_ref[i] = total
    at_odd = flags[X_ODD] > 0
    for k in range(WIDE):
        lo, hi = f_ref[k], f_ref[half - WIDE + k]
        to_even[k] = jnp.where(at_odd, lo, hi)
        to_odd[k] = jnp.where(at_odd, hi, lo)


def put_both(at_odd, even_ref, odd_ref, index, lo, hi):
    even_ref[index] = jnp.where(at_odd, lo, hi)
    odd_ref[index] = jnp.where(at_odd, hi, lo)


def mid_pack(flags, w_ref, d_ref, x_even, x_odd):
    nx = d_ref.shape[0]
    at_odd = flags[X_ODD] > 0

    @pl.loop(0, 26)
    def _(o):
        for k in range(2):
            lo, hi = w_ref[o, k].astype(F32), w_ref[o, nx - 2 + k].astype(F32)
            put_both(at_odd, x_even, x_odd, o * 2 + k, lo, hi)

    for k in range(WIDE):
        put_both(at_odd, x_even, x_odd, 52 + k, d_ref[k], d_ref[nx - WIDE + k])


def layer_beyond(flags, even, odd, index, below):
    at_odd = flags[X_ODD] > 0
    first, second = (even, odd) if below else (odd, even)
    return jnp.where(at_odd, first[index], second[index])


def mid_pack_y(flags, w_ref, d_ref, x_even, x_odd, to_even, to_odd):
    nx, ny = d_ref.shape[:2]
    at_odd = flags[Y_ODD] > 0

    def put_row(place, r, lo, hi):
        put_both(at_odd, to_even, to_odd, (place, slice(r, r + 1), slice(None)), lo, hi)

    @pl.loop(0, 26)
    def _(o):
        for x in range(nx):
            layer = w_ref[o, x].astype(F32)
            for k in range(2):
                put_row(o * 2 + k, x, layer[k : k + 1], layer[ny - 2 + k : ny - 1 + k])

    for k in range(WIDE):
        for x in range(nx):
            r = ny - WIDE + k
            put_row(52 + k, x, d_ref[x, k : k + 1, :], d_ref[x, r : r + 1, :])

    @pl.loop(0, 26)
    def _(o):
        for e in range(4):
            layer = layer_beyond(flags, x_even, x_odd, o * 2 + e % 2, e < 2)
            for k in range(2):
                lo, hi = layer[k : k + 1], layer[ny - 2 + k : ny - 1 + k]
                put_row(SLABS + o, k * 4 + e, lo, hi)

    for e in range(2 * WIDE):
        layer = layer_beyond(flags, x_even, x_odd, 52 + e % WIDE, e < WIDE)
        for k in range(WIDE):
            r = ny - WIDE + k
            put_row(SLABS + 26 + k, e, layer[k : k + 1], layer[r : r + 1])


def mid_assemble(flags, w_ref, d_ref, x_even, x_odd, y_even, y_odd, w_out, d_out, t_ref):
    nx, ny, nz = d_ref.shape
    at_odd = flags[Y_ODD] > 0
    t_ref[...] = jnp.zeros(t_ref.shape, F32)

    def put(o, x, layer, place, r):
        t_ref[x + 2, 3 : 3 + ny, :] = layer
        for k in range(2):
            index = (place(k), slice(r(k), r(k) + 1), slice(None))
            even, odd = y_even[index], y_odd[index]
            t_ref[x + 2, 1 + k : 2 + k, :] = jnp.where(at_odd, even, odd)
            t_ref[x + 2, 3 + ny + k : 4 + ny + k, :] = jnp.where(at_odd, odd, even)
        w_out[o, x + 2] = t_ref[x + 2].astype(w_out.dtype)

    @pl.loop(0, 26)
    def _(o):
        for x in range(nx):
            put(o, x, w_ref[o, x].astype(F32), lambda k: o * 2 + k, lambda k: x)
        for e, x in enumerate((-2, -1, nx, nx + 1)):
            layer = layer_beyond(flags, x_even, x_odd, o * 2 + e % 2, e < 2)
            put(o, x, layer, lambda k: SLABS + o, lambda k: k * 4 + e)

    d_out[...] = jnp.ones(d_out.shape, F32)
    for x in range(-WIDE, nx + WIDE):
        r = x + WIDE
        if 0 <= x < nx:
            layer, place, e = d_ref[x], 52, x
        else:
            e = r if x < 0 else r - nx
            layer, place = layer_beyond(flags, x_even, x_odd, 52 + e % WIDE, x < 0), SLABS + 26
        d_out[r, 3 : 3 + ny, :] = layer
        for k in range(WIDE):
            even, odd = y_even[place + k, e : e + 1, :], y_odd[place + k, e : e + 1, :]
            d_out[r, k : k + 1, :] = jnp.where(at_odd, even, odd)
            d_out[r, 3 + ny + k : 4 + ny + k, :] = jnp.where(at_odd, odd, even)


def swap_blocks(values):
    n, lanes = values.shape
    width = lanes // n
    wide = jnp.broadcast_to(values[None], (n, n, lanes))
    wide = jnp.where(iota(wide.shape, 2) // width == iota(wide.shape, 0), wide, 0.0)
    spread = jnp.where(
        iota((lanes, lanes), 0) % width == iota((lanes, lanes), 1) % width, 1.0, 0.0
    ).astype(F32)
    moved = dot_right(wide.reshape(n * n, lanes), spread).reshape(n, n, lanes)
    moved = jnp.where(iota(moved.shape, 2) // width == iota(moved.shape, 1), moved, 0.0)
    return jnp.sum(moved, axis=1)


def mid_rounds(
    flags,
    places,
    fx_ref,
    fy_even,
    fy_odd,
    d_ref,
    w_ref,
    mid_out,
    src_out,
    slot_out,
    f_ref,
    v_ref,
    s_ref,
    p_ref,
):
    ex, ey, nz = f_ref.shape
    ny = fx_ref.shape[1]
    nx = ex - 2 * WIDE
    row = iota((ey, nz), 0)

    def inside(x, reach):
        lo = jnp.where(flags[Y_LO] > 0, WIDE - reach, WIDE)
        hi = jnp.where(flags[Y_HI] > 0, WIDE + ny + reach, WIDE + ny)
        ok = (row >= lo) & (row < hi)
        if x < 0:
            ok = ok & (flags[X_LO] > 0)
        if x >= nx:
            ok = ok & (flags[X_HI] > 0)
        return ok

    for r in range(ex):
        f_ref[r] = jnp.zeros((ey, nz), F32)
        f_ref[r, WIDE : WIDE + ny, :] = fx_ref[r]
        even, odd = fy_even[r], fy_odd[r]
        f_ref[r, 0:WIDE, :] = jnp.where(flags[Y_ODD] > 0, even, odd)
        f_ref[r, WIDE + ny : 2 * WIDE + ny, :] = jnp.where(flags[Y_ODD] > 0, odd, even)
        v_ref[r] = jnp.where(inside(r - WIDE, WIDE), OMEGA * f_ref[r] / d_ref[r], 0.0)

    def spread(reach):
        for r in range(WIDE - reach, WIDE + nx + reach):
            layer = v_ref[r]
            for c in (-1, 0, 1):
                along = shift_z(layer, c)
                for b in (-1, 0, 1):
                    s_ref[(b + 1) * 3 + c + 1, r] = shift_y(along, b)

    def leftover(r):
        total = f_ref[r] - d_ref[r] * v_ref[r]
        for o, (a, b, c) in enumerate(OFFSETS):
            total = total + w_ref[o, r - 1].astype(F32) * s_ref[(b + 1) * 3 + c + 1, r + a]
        return total

    for reach in (2, 1):
        spread(reach + 1)
        for r in range(WIDE - reach, WIDE + nx + reach):
            new = v_ref[r] + OMEGA * leftover(r) / d_ref[r]
            v_ref[r] = jnp.where(inside(r - WIDE, reach), new, 0.0)
    for x in range(nx):
        mid_out[x] = v_ref[WIDE + x][WIDE : WIDE + ny]
    spread(1)
    for i in range(nx // 2):
        r = WIDE + 2 * i
        p_ref[i * ey : (i + 1) * ey, :] = leftover(r) + leftover(r + 1)

    half = ny // 2
    rows = nx // 2 * half
    out_row = iota((rows, nx // 2 * ey), 0)
    in_row = iota((rows, nx // 2 * ey), 1)
    first = (out_row // half) * ey + WIDE + 2 * (out_row % half)
    left_sum = jnp.where((in_row == first) | (in_row == first + 1), 1.0, 0.0).astype(F32)
    source = dot_right(dot_left(left_sum, p_ref[...]), pair_sum_right(nz, HALVING))
    src_out[...] = source
    blocked = swap_blocks(source)
    slot_out[...] = jnp.zeros(slot_out.shape, F32)
    for k in range(blocked.shape[0]):
        slot_out[pl.ds(places[k], 1), :] = blocked[k : k + 1]


def solve_blocks(m_ref, a_ref, out_ref):
    slots, cells = a_ref.shape
    lane = iota((cells, cells), 1)
    columns = jnp.zeros((cells, cells), F32)
    for q in range(slots):
        product = jnp.sum(m_ref[q] * a_ref[q : q + 1, :], axis=1, keepdims=True)
        columns = jnp.where(lane == q, product, columns)
    out_ref[...] = columns.T[0:slots]


def finish(places, back_ref, src_ref, dc_ref, wc_ref, cor_out, res_out, c_ref):
    blocks, cells = c_ref.shape
    nx, half = cor_out.shape[:2]
    rows = nx * half
    for k in range(blocks):
        c_ref[k : k + 1, :] = back_ref[pl.ds(places[k], 1), :]
    correction = swap_blocks(c_ref[...])
    source = src_ref[...]
    grid_row = iota(source.shape, 0)
    width = cells // blocks
    zpos = iota(source.shape, 1) % width
    residual = source - dc_ref[...] * correction
    for o, (a, b, c) in enumerate(OFFSETS):
        moved = correction
        if c:
            moved = pltpu.roll(moved, (-c) % cells, 1)
            moved = jnp.where(zpos == (0 if c < 0 else width - 1), 0.0, moved)
        if a or b:
            moved = pltpu.roll(moved, (-(a * half + b)) % rows, 0)
            y, x = grid_row % half + b, grid_row // half + a
            ok = (y >= 0) & (y < half) & (x >= 0) & (x < nx)
            moved = jnp.where(ok, moved, 0.0)
        residual = residual + wc_ref[o].astype(F32) * moved
    for x in range(nx):
        cor_out[x] = correction[x * half : (x + 1) * half]
        res_out[x] = residual[x * half : (x + 1) * half]


def block_ranks(owners):
    same = owners[:, None] == owners[None, :]
    count = owners.shape[0]
    earlier = jnp.arange(count)[None, :] < jnp.arange(count)[:, None]
    return jnp.sum((same & earlier).astype(jnp.int32), axis=-1)


def call(body, outs, ins=None, **more):
    flops = more.pop("flops", 1_000_000)
    size = more.pop("size", 1_000_000)
    limit = more.pop("limit", VMEM_LIMIT)
    return pl.pallas_call(
        body,
        out_shape=outs,
        cost_estimate=pl.CostEstimate(flops=flops, bytes_accessed=size, transcendentals=0),
        compiler_params=pltpu.CompilerParams(vmem_limit_bytes=limit),
        **more,
    )


def pairs(axis):
    size = lax.axis_size(axis)
    even = [(i, i ^ 1) for i in range(size)]
    odd = [(i, (i + 1) % size if i % 2 else (i - 1) % size) for i in range(size)]
    return even, odd


def exchange(axis, to_even, to_odd):
    even, odd = pairs(axis)
    return lax.ppermute(to_even, axis, even), lax.ppermute(to_odd, axis, odd)


def shards(
    rhs_fine,
    diag_fine,
    coup_fine,
    diag_mid,
    coup_mid,
    diag_coarse,
    coup_coarse,
    owner_map,
    inverse_blocks,
):
    nx, ny, nz = rhs_fine.shape
    g, d = lax.axis_index("group"), lax.axis_index("dev")
    n_group, n_dev = lax.axis_size("group"), lax.axis_size("dev")
    flags = jnp.stack([g > 0, g < n_group - 1, d > 0, d < n_dev - 1, g % 2 > 0, d % 2 > 0])
    slots, cells = inverse_blocks.shape[2], inverse_blocks.shape[3]
    owners = owner_map.reshape(-1)
    places = owners * (slots // n_dev) + block_ranks(owners)
    flags = flags.astype(jnp.int32)
    masks = jnp.broadcast_to(flags.astype(F32)[:, None], (6, rhs_fine.shape[2]))
    flags, masks = lax.optimization_barrier((flags, masks))

    def on(place, width=nz):
        return masks[place : place + 1, :width] > 0.5

    def by_parity(parity, lo, hi):
        at_odd = on(parity, lo.shape[-1])
        return jnp.where(at_odd, lo, hi), jnp.where(at_odd, hi, lo)

    scratch = [pltpu.VMEM((9, nx + 2, ny, nz), F32)]
    fine = sds((nx, ny, nz))
    faces = sds((4, ny, nz))
    heavy = dict(flops=60 * nx * ny * nz, size=coup_fine.size * 2 + 4 * rhs_fine.size * 4)
    one_face = sds((ny, nz))

    def stage(values_lo, values_hi, ends):
        lo_halo, hi_halo = jnp.where(on(X_ODD), *ends), jnp.where(on(X_ODD), *ends[::-1])
        lo_halo = jnp.where(on(X_LO), lo_halo, 0.0)
        hi_halo = jnp.where(on(X_HI), hi_halo, 0.0)
        to_lo = jnp.concatenate([lo_halo[:1], values_lo, hi_halo[:1]], axis=0)
        to_hi = jnp.concatenate([lo_halo[-1:], values_hi, hi_halo[-1:]], axis=0)
        return by_parity(Y_ODD, to_lo, to_hi)

    hx, hy, hz = nx // 2, ny // 2, nz // 2

    faces_now = [OMEGA / diag_fine[x] * rhs_fine[x] for x in (0, nx - 1)]
    ends = exchange("group", *by_parity(X_ODD, *faces_now))
    start, q, *new = call(
        fine_start,
        (fine, fine) + (one_face,) * 2,
        in_specs=[VMEM] * 2,
        out_specs=(VMEM,) * 4,
        flops=LONG,
    )(rhs_fine, diag_fine)
    ends, new = lax.optimization_barrier((ends, new))
    messages = stage(new[0], new[1], ends)
    messages, late = lax.optimization_barrier((messages, flags))
    v, v_faces, q_faces, w_faces = call(
        fine_first,
        (fine, faces, faces, sds((4, 9, ny, nz), coup_fine.dtype)),
        in_specs=[SMEM] + [VMEM] * 3,
        out_specs=(VMEM,) * 4,
        scratch_shapes=scratch + [pltpu.VMEM((2, 9, nx, nz), F32)],
        **heavy,
    )(late, start, q, coup_fine)
    halo = ends + exchange("dev", *messages)
    fix = call(
        fine_halo,
        (one_face,) * 6,
        in_specs=[SMEM] + [VMEM] * 7,
        out_specs=(VMEM,) * 6,
    )
    *new, x_even, x_odd = fix(flags, *halo, w_faces, v_faces, q_faces)

    ends = exchange("group", x_even, x_odd)
    v, v_faces = call(
        fine_next,
        (fine, faces),
        in_specs=[VMEM] * 8,
        out_specs=(VMEM,) * 2,
        scratch_shapes=scratch,
        **heavy,
    )(v, *new, start, q, coup_fine)
    ends, v_faces, new = lax.optimization_barrier((ends, v_faces, new))
    messages = stage(new[2], new[3], ends)
    messages, late = lax.optimization_barrier((messages, flags))
    halo = ends + exchange("dev", *messages)
    slabs = sds((SLABS, hy, hz))
    wx = call(
        mid_pack,
        (slabs, slabs),
        in_specs=[SMEM] + [VMEM] * 2,
        out_specs=(VMEM,) * 2,
        flops=LONG,
    )(late, coup_mid, diag_mid)
    halo, _ = lax.optimization_barrier((halo, wx))
    wx = exchange("group", *wx)
    *new, x_even, x_odd = fix(flags, *halo, w_faces, v_faces, q_faces)

    ends = exchange("group", x_even, x_odd)
    fine_iterate, g_mid = call(
        fine_last,
        (fine, sds((hx, hy, hz))),
        in_specs=[VMEM] * 8,
        out_specs=(VMEM,) * 2,
        scratch_shapes=scratch + [pltpu.VMEM((hx * ny, nz), F32)],
    )(v, *new, start, q, coup_fine)
    ends, g_mid, new = lax.optimization_barrier((ends, g_mid, new))
    messages = stage(new[2], new[3], ends)
    messages, late = lax.optimization_barrier((messages, flags))
    halo = ends + exchange("dev", *messages)
    strips = sds((SLABS + 26 + WIDE, hx, hz))
    wy = call(
        mid_pack_y,
        (strips, strips),
        in_specs=[SMEM] + [VMEM] * 4,
        out_specs=(VMEM,) * 2,
        flops=LONG,
    )(late, coup_mid, diag_mid, *wx)
    halo, wy = lax.optimization_barrier((halo, wy))
    wy = exchange("dev", *wy)
    f_mid, fx_even, fx_odd = call(
        fine_halo_last,
        (sds((hx, hy, hz)), sds((WIDE, hy, hz)), sds((WIDE, hy, hz))),
        in_specs=[SMEM] + [VMEM] * 6,
        out_specs=(VMEM,) * 3,
        scratch_shapes=[pltpu.VMEM((4 * ny, nz), F32)],
    )(flags, *halo, w_faces, g_mid)

    fx_even, fx_odd = exchange("group", fx_even, fx_odd)
    at_odd = on(X_ODD, hz)
    fx_lo, fx_hi = jnp.where(at_odd, fx_even, fx_odd), jnp.where(at_odd, fx_odd, fx_even)
    fx = jnp.concatenate([fx_lo, f_mid, fx_hi], axis=0)
    fy = exchange("dev", *by_parity(Y_ODD, fx[:, :WIDE], fx[:, hy - WIDE :]))
    ex, ey = hx + 2 * WIDE, 16
    w_wide, d_wide = call(
        mid_assemble,
        (sds((26, hx + 4, ey, hz), coup_mid.dtype), sds((ex, ey, hz))),
        in_specs=[SMEM] + [VMEM] * 6,
        out_specs=(VMEM,) * 2,
        scratch_shapes=[pltpu.VMEM((hx + 4, ey, hz), F32)],
        flops=LONG,
    )(flags, coup_mid, diag_mid, *wx, *wy)
    qx, qy, qz = hx // 2, hy // 2, hz // 2
    mid_iterate, source, outgoing = call(
        mid_rounds,
        (sds((hx, hy, hz)), sds((qx * qy, qz)), sds((slots, cells))),
        in_specs=[SMEM] * 2 + [VMEM] * 5,
        out_specs=(VMEM,) * 3,
        scratch_shapes=[
            pltpu.VMEM((ex, ey, hz), F32),
            pltpu.VMEM((ex, ey, hz), F32),
            pltpu.VMEM((9, ex, ey, hz), F32),
            pltpu.VMEM((hx // 2 * ey, hz), F32),
        ],
        flops=20_000_000,
    )(flags, places, fx, *fy, d_wide, w_wide)

    arrived = lax.all_to_all(outgoing, "dev", split_axis=0, concat_axis=0, tiled=True)
    owned = call(solve_blocks, sds((slots, cells)), in_specs=[VMEM] * 2, out_specs=VMEM)(
        inverse_blocks.reshape(slots, cells, cells), arrived
    )
    returned = lax.all_to_all(owned, "dev", split_axis=0, concat_axis=0, tiled=True)
    correction, residual = call(
        finish,
        (sds((qx, qy, qz)), sds((qx, qy, qz))),
        in_specs=[SMEM] + [VMEM] * 4,
        out_specs=(VMEM,) * 2,
        scratch_shapes=[pltpu.VMEM((owners.shape[0], cells), F32)],
    )(
        places,
        returned,
        source,
        diag_coarse.reshape(qx * qy, qz),
        coup_coarse.reshape(26, qx * qy, qz),
    )
    return fine_iterate, mid_iterate, correction, residual


def solution(mesh):
    return jax.shard_map(
        shards,
        mesh=mesh,
        in_specs=(
            P("group", "dev", None),
            P("group", "dev", None),
            P(None, "group", "dev", None),
            P("group", "dev", None),
            P(None, "group", "dev", None),
            P("group", "dev", None),
            P(None, "group", "dev", None),
            P("group", "dev", None, None),
            P("group", "dev", None, None, None),
        ),
        out_specs=(
            P("group", "dev", None),
            P("group", "dev", None),
            P("group", "dev", None),
            P("group", "dev", None),
        ),
        check_vma=False,
    )
```

```python
import jax
import jax.numpy as jnp
from jax import lax
from jax.experimental import pallas as pl
from jax.experimental.pallas import tpu as pltpu
from jax.sharding import PartitionSpec as P

OMEGA = 0.8
HALVING = 0.5
OFFSETS = [
    (a, b, c)
    for a in (-1, 0, 1)
    for b in (-1, 0, 1)
    for c in (-1, 0, 1)
    if (a, b, c) != (0, 0, 0)
]
TO_YLO = [OFFSETS.index((a, -1, c)) for a in (-1, 0, 1) for c in (-1, 0, 1)]
TO_YHI = [OFFSETS.index((a, 1, c)) for a in (-1, 0, 1) for c in (-1, 0, 1)]
F32 = jnp.float32
VMEM_LIMIT = 20 * 1024 * 1024
XB = 4
WIDE = 3
SLABS = 52 + WIDE
X_LO, X_HI, Y_LO, Y_HI, X_ODD, Y_ODD = range(6)
LONG = 30_000_000_000
VMEM = pl.BlockSpec(memory_space=pltpu.VMEM)
SMEM = pl.BlockSpec(memory_space=pltpu.SMEM)


def sds(shape, dtype=F32):
    return jax.ShapeDtypeStruct(shape, dtype)


def iota(shape, dim):
    return lax.broadcasted_iota(jnp.int32, shape, dim)


def shift_z(v, c):
    if c == 0:
        return v
    n, dim = v.shape[-1], v.ndim - 1
    edge = 0 if c < 0 else n - 1
    return jnp.where(iota(v.shape, dim) == edge, 0.0, pltpu.roll(v, (-c) % n, dim))


def shift_y(v, b):
    if b == 0:
        return v
    n, dim = v.shape[-2], v.ndim - 2
    edge = 0 if b < 0 else n - 1
    return jnp.where(iota(v.shape, dim) == edge, 0.0, pltpu.roll(v, (-b) % n, dim))


def pair_sum_right(n, scale):
    return jnp.where((iota((n, n // 2), 0) >> 1) == iota((n, n // 2), 1), scale, 0.0).astype(F32)


def pair_sum_left(n):
    return jnp.where((iota((n // 2, n), 1) >> 1) == iota((n // 2, n), 0), 1.0, 0.0).astype(F32)


def parts_of(v):
    first = v.astype(jnp.bfloat16)
    rest = v - first.astype(F32)
    second = rest.astype(jnp.bfloat16)
    return first, second, (rest - second.astype(F32)).astype(jnp.bfloat16)


def dot_right(v, m):
    m = m.astype(jnp.bfloat16)
    return sum(jnp.dot(part, m, preferred_element_type=F32) for part in parts_of(v)[::-1])


def dot_left(m, v):
    m = m.astype(jnp.bfloat16)
    return sum(jnp.dot(m, part, preferred_element_type=F32) for part in parts_of(v)[::-1])


def put_versions(s_ref, x, layer):
    for c in (-1, 0, 1):
        along = shift_z(layer, c)
        for b in (-1, 0, 1):
            s_ref[(b + 1) * 3 + c + 1, x + 1] = shift_y(along, b)


def neighbours(w_ref, s_ref, first, at):
    total = [None] * XB
    for b in (-1, 0, 1):
        for c in (-1, 0, 1):
            k = (b + 1) * 3 + c + 1
            layers = [s_ref[k, first + r, :, at] for r in range(XB + 2)]
            for a in (-1, 0, 1):
                if (a, b, c) == (0, 0, 0):
                    continue
                o = OFFSETS.index((a, b, c))
                for i in range(XB):
                    term = w_ref[o, first + i, :, at].astype(F32) * layers[i + 1 + a]
                    total[i] = term if total[i] is None else total[i] + term
    return total


def lane_chunks(n):
    return [slice(k, k + 128) for k in range(0, n, 128)]


def zero_rims(s_ref):
    for edge in (0, s_ref.shape[1] - 1):
        for k in range(9):
            s_ref[k, edge] = jnp.zeros(s_ref.shape[2:], F32)


def patched(v_ref, new, x, last):
    xlo, xhi, ylo, yhi = new
    layer = v_ref[x]
    row = iota(layer.shape, 0)
    layer = jnp.where(row == 0, ylo[pl.ds(x, 1), :], layer)
    layer = jnp.where(row == layer.shape[0] - 1, yhi[pl.ds(x, 1), :], layer)
    layer = jnp.where(x == 0, xlo[...], layer)
    return jnp.where(x == last, xhi[...], layer)


def put_faces(faces_ref, v_ref):
    nx, ny = v_ref.shape[:2]
    faces_ref[0] = v_ref[0]
    faces_ref[1] = v_ref[nx - 1]
    for x in range(nx):
        faces_ref[2, x : x + 1, :] = v_ref[x, 0:1, :]
        faces_ref[3, x : x + 1, :] = v_ref[x, ny - 1 : ny, :]


def put_next(v_ref, start_ref, q_ref, w_ref, s_ref, j):
    for at in lane_chunks(v_ref.shape[2]):
        for i, total in enumerate(neighbours(w_ref, s_ref, j * XB, at)):
            x = j * XB + i
            centre = (1.0 - OMEGA) * s_ref[4, x + 1, :, at]
            v_ref[x, :, at] = centre + start_ref[x, :, at] + q_ref[x, :, at] * total


def fine_start(f_ref, d_ref, start_ref, q_ref, ylo, yhi):
    nx, ny = f_ref.shape[:2]

    @pl.loop(0, nx)
    def _(x):
        q = OMEGA / d_ref[x]
        q_ref[x] = q
        start_ref[x] = q * f_ref[x]

    for x in range(nx):
        ylo[x : x + 1, :] = start_ref[x, 0:1, :]
        yhi[x : x + 1, :] = start_ref[x, ny - 1 : ny, :]


def fine_first(
    _, start_ref, q_ref, w_ref, v_ref, faces_ref, qfaces_ref, wfaces_ref, s_ref, wy_ref
):
    nx, ny = v_ref.shape[:2]
    zero_rims(s_ref)

    @pl.loop(0, nx)
    def _(x):
        put_versions(s_ref, x, start_ref[x])

    @pl.loop(0, nx // XB)
    def _(j):
        put_next(v_ref, start_ref, q_ref, w_ref, s_ref, j)
        for i in range(XB):
            x = j * XB + i
            for k in range(9):
                wy_ref[0, k, pl.ds(x, 1), :] = w_ref[TO_YLO[k], x].astype(F32)[0:1, :]
                wy_ref[1, k, pl.ds(x, 1), :] = w_ref[TO_YHI[k], x].astype(F32)[ny - 1 : ny, :]

    wfaces_ref[0] = w_ref[0:9, 0]
    wfaces_ref[1] = w_ref[17:26, nx - 1]
    for k in range(9):
        wfaces_ref[2, k] = wy_ref[0, k].astype(wfaces_ref.dtype)
        wfaces_ref[3, k] = wy_ref[1, k].astype(wfaces_ref.dtype)
    put_faces(faces_ref, v_ref)
    put_faces(qfaces_ref, q_ref)


def fine_next(v_ref, xlo, xhi, ylo, yhi, start_ref, q_ref, w_ref, out_ref, faces_ref, s_ref):
    nx = v_ref.shape[0]
    zero_rims(s_ref)

    @pl.loop(0, nx)
    def _(x):
        put_versions(s_ref, x, patched(v_ref, (xlo, xhi, ylo, yhi), x, nx - 1))

    @pl.loop(0, nx // XB)
    def _(j):
        put_next(out_ref, start_ref, q_ref, w_ref, s_ref, j)

    put_faces(faces_ref, out_ref)


def fine_last(v_ref, xlo, xhi, ylo, yhi, start_ref, q_ref, w_ref, out_ref, g_ref, s_ref, p_ref):
    nx, ny, nz = v_ref.shape
    zero_rims(s_ref)

    @pl.loop(0, nx)
    def _(x):
        layer = patched(v_ref, (xlo, xhi, ylo, yhi), x, nx - 1)
        out_ref[x] = layer
        put_versions(s_ref, x, layer)

    @pl.loop(0, nx // XB)
    def _(j):
        for at in lane_chunks(nz):
            total = neighbours(w_ref, s_ref, j * XB, at)
            for i in range(XB):
                x = j * XB + i
                own = start_ref[x, :, at] - OMEGA * s_ref[4, x + 1, :, at]
                total[i] = total[i] + own / q_ref[x, :, at]
            for i in range(0, XB, 2):
                row = pl.multiple_of((j * (XB // 2) + i // 2) * ny, ny)
                p_ref[pl.ds(row, ny), at] = total[i] + total[i + 1]

    rows = dot_left(pair_sum_left(nx // 2 * ny), p_ref[...])
    g_ref[...] = dot_right(rows, pair_sum_right(nz, HALVING)).reshape(g_ref.shape)


def sides(flags, even, odd, lo, hi, parity):
    at_odd = flags[parity] > 0
    below = jnp.where(at_odd, even, odd)
    above = jnp.where(at_odd, odd, even)
    return jnp.where(flags[lo] > 0, below, 0.0), jnp.where(flags[hi] > 0, above, 0.0)


def halo_terms(flags, x_even, x_odd, y_even, y_odd, w_ref):
    xs, ys = [], []
    n = x_even.shape[0]
    x_sides = sides(flags, x_even[...], x_odd[...], X_LO, X_HI, X_ODD)
    y_sides = sides(flags, y_even[...], y_odd[...], Y_LO, Y_HI, Y_ODD)
    for side, halo in enumerate(x_sides):
        total = None
        for c in (-1, 0, 1):
            along = shift_z(halo, c)
            for b in (-1, 0, 1):
                term = w_ref[side, (b + 1) * 3 + c + 1].astype(F32) * shift_y(along, b)
                total = term if total is None else total + term
        xs.append(total)
    for side, halo in enumerate(y_sides):
        total = None
        for c in (-1, 0, 1):
            along = shift_z(halo, c)
            for a in (-1, 0, 1):
                term = w_ref[2 + side, (a + 1) * 3 + c + 1].astype(F32) * along[1 + a : 1 + a + n]
                total = term if total is None else total + term
        ys.append(total)
    return xs, ys


def fine_halo(flags, x_even, x_odd, y_even, y_odd, w_ref, faces_ref, q_ref, *outs):
    xs, ys = halo_terms(flags, x_even, x_odd, y_even, y_odd, w_ref)
    n = xs[0].shape[0]
    row = iota(xs[0].shape, 0)

    def crossed(own, others, place):
        own = jnp.where(row == 0, own + others[0][place : place + 1], own)
        return jnp.where(row == n - 1, own + others[1][place : place + 1], own)

    sums = [
        crossed(xs[0], ys, 0),
        crossed(xs[1], ys, n - 1),
        crossed(ys[0], xs, 0),
        crossed(ys[1], xs, n - 1),
    ]
    new = [faces_ref[k] + q_ref[k] * sums[k] for k in range(4)]
    for k in range(4):
        outs[k][...] = new[k]
    at_odd = flags[X_ODD] > 0
    outs[4][...] = jnp.where(at_odd, new[0], new[1])
    outs[5][...] = jnp.where(at_odd, new[1], new[0])


def fine_halo_last(
    flags, x_even, x_odd, y_even, y_odd, w_ref, g_ref, f_ref, to_even, to_odd, t_ref
):
    xs, ys = halo_terms(flags, x_even, x_odd, y_even, y_odd, w_ref)
    n, nz = xs[0].shape
    for k, part in enumerate(xs + ys):
        t_ref[k * n : (k + 1) * n, :] = part
    rows = dot_left(pair_sum_left(4 * n), t_ref[...])
    half = n // 2
    coarse = dot_right(rows, pair_sum_right(nz, HALVING))
    row = iota((half, nz // 2), 0)
    for i in range(half):
        total = g_ref[i]
        total = total + jnp.where(row == 0, coarse[2 * half + i : 2 * half + i + 1], 0.0)
        total = total + jnp.where(row == half - 1, coarse[3 * half + i : 3 * half + i + 1], 0.0)
        if i == 0:
            total = total + coarse[0:half]
        if i == half - 1:
            total = total + coarse[half : 2 * half]
        f_ref[i] = total
    at_odd = flags[X_ODD] > 0
    for k in range(WIDE):
        lo, hi = f_ref[k], f_ref[half - WIDE + k]
        to_even[k] = jnp.where(at_odd, lo, hi)
        to_odd[k] = jnp.where(at_odd, hi, lo)


def put_both(at_odd, even_ref, odd_ref, index, lo, hi):
    even_ref[index] = jnp.where(at_odd, lo, hi)
    odd_ref[index] = jnp.where(at_odd, hi, lo)


def mid_pack(flags, w_ref, d_ref, x_even, x_odd):
    nx = d_ref.shape[0]
    at_odd = flags[X_ODD] > 0

    @pl.loop(0, 26)
    def _(o):
        for k in range(2):
            lo, hi = w_ref[o, k].astype(F32), w_ref[o, nx - 2 + k].astype(F32)
            put_both(at_odd, x_even, x_odd, o * 2 + k, lo, hi)

    for k in range(WIDE):
        put_both(at_odd, x_even, x_odd, 52 + k, d_ref[k], d_ref[nx - WIDE + k])


def layer_beyond(flags, even, odd, index, below):
    at_odd = flags[X_ODD] > 0
    first, second = (even, odd) if below else (odd, even)
    return jnp.where(at_odd, first[index], second[index])


def mid_pack_y(flags, w_ref, d_ref, x_even, x_odd, to_even, to_odd):
    nx, ny = d_ref.shape[:2]
    at_odd = flags[Y_ODD] > 0

    def put_row(place, r, lo, hi):
        put_both(at_odd, to_even, to_odd, (place, slice(r, r + 1), slice(None)), lo, hi)

    @pl.loop(0, 26)
    def _(o):
        for x in range(nx):
            layer = w_ref[o, x].astype(F32)
            for k in range(2):
                put_row(o * 2 + k, x, layer[k : k + 1], layer[ny - 2 + k : ny - 1 + k])

    for k in range(WIDE):
        for x in range(nx):
            r = ny - WIDE + k
            put_row(52 + k, x, d_ref[x, k : k + 1, :], d_ref[x, r : r + 1, :])

    @pl.loop(0, 26)
    def _(o):
        for e in range(4):
            layer = layer_beyond(flags, x_even, x_odd, o * 2 + e % 2, e < 2)
            for k in range(2):
                lo, hi = layer[k : k + 1], layer[ny - 2 + k : ny - 1 + k]
                put_row(SLABS + o, k * 4 + e, lo, hi)

    for e in range(2 * WIDE):
        layer = layer_beyond(flags, x_even, x_odd, 52 + e % WIDE, e < WIDE)
        for k in range(WIDE):
            r = ny - WIDE + k
            put_row(SLABS + 26 + k, e, layer[k : k + 1], layer[r : r + 1])


def mid_assemble(flags, w_ref, d_ref, x_even, x_odd, y_even, y_odd, w_out, d_out, t_ref):
    nx, ny, nz = d_ref.shape
    at_odd = flags[Y_ODD] > 0
    t_ref[...] = jnp.zeros(t_ref.shape, F32)

    def put(o, x, layer, place, r):
        t_ref[x + 2, 3 : 3 + ny, :] = layer
        for k in range(2):
            index = (place(k), slice(r(k), r(k) + 1), slice(None))
            even, odd = y_even[index], y_odd[index]
            t_ref[x + 2, 1 + k : 2 + k, :] = jnp.where(at_odd, even, odd)
            t_ref[x + 2, 3 + ny + k : 4 + ny + k, :] = jnp.where(at_odd, odd, even)
        w_out[o, x + 2] = t_ref[x + 2].astype(w_out.dtype)

    @pl.loop(0, 26)
    def _(o):
        for x in range(nx):
            put(o, x, w_ref[o, x].astype(F32), lambda k: o * 2 + k, lambda k: x)
        for e, x in enumerate((-2, -1, nx, nx + 1)):
            layer = layer_beyond(flags, x_even, x_odd, o * 2 + e % 2, e < 2)
            put(o, x, layer, lambda k: SLABS + o, lambda k: k * 4 + e)

    d_out[...] = jnp.ones(d_out.shape, F32)
    for x in range(-WIDE, nx + WIDE):
        r = x + WIDE
        if 0 <= x < nx:
            layer, place, e = d_ref[x], 52, x
        else:
            e = r if x < 0 else r - nx
            layer, place = layer_beyond(flags, x_even, x_odd, 52 + e % WIDE, x < 0), SLABS + 26
        d_out[r, 3 : 3 + ny, :] = layer
        for k in range(WIDE):
            even, odd = y_even[place + k, e : e + 1, :], y_odd[place + k, e : e + 1, :]
            d_out[r, k : k + 1, :] = jnp.where(at_odd, even, odd)
            d_out[r, 3 + ny + k : 4 + ny + k, :] = jnp.where(at_odd, odd, even)


def swap_blocks(values):
    n, lanes = values.shape
    width = lanes // n
    wide = jnp.broadcast_to(values[None], (n, n, lanes))
    wide = jnp.where(iota(wide.shape, 2) // width == iota(wide.shape, 0), wide, 0.0)
    spread = jnp.where(
        iota((lanes, lanes), 0) % width == iota((lanes, lanes), 1) % width, 1.0, 0.0
    ).astype(F32)
    moved = dot_right(wide.reshape(n * n, lanes), spread).reshape(n, n, lanes)
    moved = jnp.where(iota(moved.shape, 2) // width == iota(moved.shape, 1), moved, 0.0)
    return jnp.sum(moved, axis=1)


def mid_rounds(
    flags,
    places,
    fx_ref,
    fy_even,
    fy_odd,
    d_ref,
    w_ref,
    mid_out,
    src_out,
    slot_out,
    f_ref,
    v_ref,
    s_ref,
    p_ref,
):
    ex, ey, nz = f_ref.shape
    ny = fx_ref.shape[1]
    nx = ex - 2 * WIDE
    row = iota((ey, nz), 0)

    def inside(x, reach):
        lo = jnp.where(flags[Y_LO] > 0, WIDE - reach, WIDE)
        hi = jnp.where(flags[Y_HI] > 0, WIDE + ny + reach, WIDE + ny)
        ok = (row >= lo) & (row < hi)
        if x < 0:
            ok = ok & (flags[X_LO] > 0)
        if x >= nx:
            ok = ok & (flags[X_HI] > 0)
        return ok

    for r in range(ex):
        f_ref[r] = jnp.zeros((ey, nz), F32)
        f_ref[r, WIDE : WIDE + ny, :] = fx_ref[r]
        even, odd = fy_even[r], fy_odd[r]
        f_ref[r, 0:WIDE, :] = jnp.where(flags[Y_ODD] > 0, even, odd)
        f_ref[r, WIDE + ny : 2 * WIDE + ny, :] = jnp.where(flags[Y_ODD] > 0, odd, even)
        v_ref[r] = jnp.where(inside(r - WIDE, WIDE), OMEGA * f_ref[r] / d_ref[r], 0.0)

    def spread(reach):
        for r in range(WIDE - reach, WIDE + nx + reach):
            layer = v_ref[r]
            for c in (-1, 0, 1):
                along = shift_z(layer, c)
                for b in (-1, 0, 1):
                    s_ref[(b + 1) * 3 + c + 1, r] = shift_y(along, b)

    def leftover(r):
        total = f_ref[r] - d_ref[r] * v_ref[r]
        for o, (a, b, c) in enumerate(OFFSETS):
            total = total + w_ref[o, r - 1].astype(F32) * s_ref[(b + 1) * 3 + c + 1, r + a]
        return total

    for reach in (2, 1):
        spread(reach + 1)
        for r in range(WIDE - reach, WIDE + nx + reach):
            new = v_ref[r] + OMEGA * leftover(r) / d_ref[r]
            v_ref[r] = jnp.where(inside(r - WIDE, reach), new, 0.0)
    for x in range(nx):
        mid_out[x] = v_ref[WIDE + x][WIDE : WIDE + ny]
    spread(1)
    for i in range(nx // 2):
        r = WIDE + 2 * i
        p_ref[i * ey : (i + 1) * ey, :] = leftover(r) + leftover(r + 1)

    half = ny // 2
    rows = nx // 2 * half
    out_row = iota((rows, nx // 2 * ey), 0)
    in_row = iota((rows, nx // 2 * ey), 1)
    first = (out_row // half) * ey + WIDE + 2 * (out_row % half)
    left_sum = jnp.where((in_row == first) | (in_row == first + 1), 1.0, 0.0).astype(F32)
    source = dot_right(dot_left(left_sum, p_ref[...]), pair_sum_right(nz, HALVING))
    src_out[...] = source
    blocked = swap_blocks(source)
    slot_out[...] = jnp.zeros(slot_out.shape, F32)
    for k in range(blocked.shape[0]):
        slot_out[pl.ds(places[k], 1), :] = blocked[k : k + 1]


def solve_blocks(m_ref, a_ref, out_ref):
    slots, cells = a_ref.shape
    lane = iota((cells, cells), 1)
    columns = jnp.zeros((cells, cells), F32)
    for q in range(slots):
        product = jnp.sum(m_ref[q] * a_ref[q : q + 1, :], axis=1, keepdims=True)
        columns = jnp.where(lane == q, product, columns)
    out_ref[...] = columns.T[0:slots]


def finish(places, back_ref, src_ref, dc_ref, wc_ref, cor_out, res_out, c_ref):
    blocks, cells = c_ref.shape
    nx, half = cor_out.shape[:2]
    rows = nx * half
    for k in range(blocks):
        c_ref[k : k + 1, :] = back_ref[pl.ds(places[k], 1), :]
    correction = swap_blocks(c_ref[...])
    source = src_ref[...]
    grid_row = iota(source.shape, 0)
    width = cells // blocks
    zpos = iota(source.shape, 1) % width
    residual = source - dc_ref[...] * correction
    for o, (a, b, c) in enumerate(OFFSETS):
        moved = correction
        if c:
            moved = pltpu.roll(moved, (-c) % cells, 1)
            moved = jnp.where(zpos == (0 if c < 0 else width - 1), 0.0, moved)
        if a or b:
            moved = pltpu.roll(moved, (-(a * half + b)) % rows, 0)
            y, x = grid_row % half + b, grid_row // half + a
            ok = (y >= 0) & (y < half) & (x >= 0) & (x < nx)
            moved = jnp.where(ok, moved, 0.0)
        residual = residual + wc_ref[o].astype(F32) * moved
    for x in range(nx):
        cor_out[x] = correction[x * half : (x + 1) * half]
        res_out[x] = residual[x * half : (x + 1) * half]


def block_ranks(owners):
    same = owners[:, None] == owners[None, :]
    count = owners.shape[0]
    earlier = jnp.arange(count)[None, :] < jnp.arange(count)[:, None]
    return jnp.sum((same & earlier).astype(jnp.int32), axis=-1)


def call(body, outs, ins=None, **more):
    flops = more.pop("flops", 1_000_000)
    size = more.pop("size", 1_000_000)
    limit = more.pop("limit", VMEM_LIMIT)
    return pl.pallas_call(
        body,
        out_shape=outs,
        cost_estimate=pl.CostEstimate(flops=flops, bytes_accessed=size, transcendentals=0),
        compiler_params=pltpu.CompilerParams(vmem_limit_bytes=limit),
        **more,
    )


def pairs(axis):
    size = lax.axis_size(axis)
    even = [(i, i ^ 1) for i in range(size)]
    odd = [(i, (i + 1) % size if i % 2 else (i - 1) % size) for i in range(size)]
    return even, odd


def exchange(axis, to_even, to_odd):
    even, odd = pairs(axis)
    return lax.ppermute(to_even, axis, even), lax.ppermute(to_odd, axis, odd)


def shards(
    rhs_fine,
    diag_fine,
    coup_fine,
    diag_mid,
    coup_mid,
    diag_coarse,
    coup_coarse,
    owner_map,
    inverse_blocks,
):
    nx, ny, nz = rhs_fine.shape
    g, d = lax.axis_index("group"), lax.axis_index("dev")
    n_group, n_dev = lax.axis_size("group"), lax.axis_size("dev")
    flags = jnp.stack([g > 0, g < n_group - 1, d > 0, d < n_dev - 1, g % 2 > 0, d % 2 > 0])
    slots, cells = inverse_blocks.shape[2], inverse_blocks.shape[3]
    owners = owner_map.reshape(-1)
    places = owners * (slots // n_dev) + block_ranks(owners)
    flags = flags.astype(jnp.int32)
    masks = jnp.broadcast_to(flags.astype(F32)[:, None], (6, rhs_fine.shape[2]))
    flags, masks = lax.optimization_barrier((flags, masks))

    def on(place, width=nz):
        return masks[place : place + 1, :width] > 0.5

    def by_parity(parity, lo, hi):
        at_odd = on(parity, lo.shape[-1])
        return jnp.where(at_odd, lo, hi), jnp.where(at_odd, hi, lo)

    scratch = [pltpu.VMEM((9, nx + 2, ny, nz), F32)]
    fine = sds((nx, ny, nz))
    faces = sds((4, ny, nz))
    heavy = dict(flops=60 * nx * ny * nz, size=coup_fine.size * 2 + 4 * rhs_fine.size * 4)
    one_face = sds((ny, nz))

    def stage(values_lo, values_hi, ends):
        lo_halo, hi_halo = jnp.where(on(X_ODD), *ends), jnp.where(on(X_ODD), *ends[::-1])
        lo_halo = jnp.where(on(X_LO), lo_halo, 0.0)
        hi_halo = jnp.where(on(X_HI), hi_halo, 0.0)
        to_lo = jnp.concatenate([lo_halo[:1], values_lo, hi_halo[:1]], axis=0)
        to_hi = jnp.concatenate([lo_halo[-1:], values_hi, hi_halo[-1:]], axis=0)
        return by_parity(Y_ODD, to_lo, to_hi)

    hx, hy, hz = nx // 2, ny // 2, nz // 2

    faces_now = [OMEGA / diag_fine[x] * rhs_fine[x] for x in (0, nx - 1)]
    ends = exchange("group", *by_parity(X_ODD, *faces_now))
    start, q, *new = call(
        fine_start,
        (fine, fine) + (one_face,) * 2,
        in_specs=[VMEM] * 2,
        out_specs=(VMEM,) * 4,
        flops=LONG,
    )(rhs_fine, diag_fine)
    ends, new = lax.optimization_barrier((ends, new))
    messages = stage(new[0], new[1], ends)
    messages, late = lax.optimization_barrier((messages, flags))
    v, v_faces, q_faces, w_faces = call(
        fine_first,
        (fine, faces, faces, sds((4, 9, ny, nz), coup_fine.dtype)),
        in_specs=[SMEM] + [VMEM] * 3,
        out_specs=(VMEM,) * 4,
        scratch_shapes=scratch + [pltpu.VMEM((2, 9, nx, nz), F32)],
        **heavy,
    )(late, start, q, coup_fine)
    halo = ends + exchange("dev", *messages)
    fix = call(
        fine_halo,
        (one_face,) * 6,
        in_specs=[SMEM] + [VMEM] * 7,
        out_specs=(VMEM,) * 6,
    )
    *new, x_even, x_odd = fix(flags, *halo, w_faces, v_faces, q_faces)

    ends = exchange("group", x_even, x_odd)
    v, v_faces = call(
        fine_next,
        (fine, faces),
        in_specs=[VMEM] * 8,
        out_specs=(VMEM,) * 2,
        scratch_shapes=scratch,
        **heavy,
    )(v, *new, start, q, coup_fine)
    ends, v_faces, new = lax.optimization_barrier((ends, v_faces, new))
    messages = stage(new[2], new[3], ends)
    messages, late = lax.optimization_barrier((messages, flags))
    halo = ends + exchange("dev", *messages)
    slabs = sds((SLABS, hy, hz))
    wx = call(
        mid_pack,
        (slabs, slabs),
        in_specs=[SMEM] + [VMEM] * 2,
        out_specs=(VMEM,) * 2,
        flops=LONG,
    )(late, coup_mid, diag_mid)
    halo, _ = lax.optimization_barrier((halo, wx))
    wx = exchange("group", *wx)
    *new, x_even, x_odd = fix(flags, *halo, w_faces, v_faces, q_faces)

    ends = exchange("group", x_even, x_odd)
    fine_iterate, g_mid = call(
        fine_last,
        (fine, sds((hx, hy, hz))),
        in_specs=[VMEM] * 8,
        out_specs=(VMEM,) * 2,
        scratch_shapes=scratch + [pltpu.VMEM((hx * ny, nz), F32)],
    )(v, *new, start, q, coup_fine)
    ends, g_mid, new = lax.optimization_barrier((ends, g_mid, new))
    messages = stage(new[2], new[3], ends)
    messages, late = lax.optimization_barrier((messages, flags))
    halo = ends + exchange("dev", *messages)
    strips = sds((SLABS + 26 + WIDE, hx, hz))
    wy = call(
        mid_pack_y,
        (strips, strips),
        in_specs=[SMEM] + [VMEM] * 4,
        out_specs=(VMEM,) * 2,
        flops=LONG,
    )(late, coup_mid, diag_mid, *wx)
    *ends, y_even, y_odd = halo
    y_even, wy = lax.optimization_barrier((y_even, wy))
    halo = (*ends, y_even, y_odd)
    wy = exchange("dev", *wy)
    f_mid, fx_even, fx_odd = call(
        fine_halo_last,
        (sds((hx, hy, hz)), sds((WIDE, hy, hz)), sds((WIDE, hy, hz))),
        in_specs=[SMEM] + [VMEM] * 6,
        out_specs=(VMEM,) * 3,
        scratch_shapes=[pltpu.VMEM((4 * ny, nz), F32)],
    )(flags, *halo, w_faces, g_mid)

    fx_even, fx_odd = exchange("group", fx_even, fx_odd)
    at_odd = on(X_ODD, hz)
    fx_lo, fx_hi = jnp.where(at_odd, fx_even, fx_odd), jnp.where(at_odd, fx_odd, fx_even)
    fx = jnp.concatenate([fx_lo, f_mid, fx_hi], axis=0)
    fy = exchange("dev", *by_parity(Y_ODD, fx[:, :WIDE], fx[:, hy - WIDE :]))
    ex, ey = hx + 2 * WIDE, 16
    w_wide, d_wide = call(
        mid_assemble,
        (sds((26, hx + 4, ey, hz), coup_mid.dtype), sds((ex, ey, hz))),
        in_specs=[SMEM] + [VMEM] * 6,
        out_specs=(VMEM,) * 2,
        scratch_shapes=[pltpu.VMEM((hx + 4, ey, hz), F32)],
        flops=LONG,
    )(flags, coup_mid, diag_mid, *wx, *wy)
    qx, qy, qz = hx // 2, hy // 2, hz // 2
    mid_iterate, source, outgoing = call(
        mid_rounds,
        (sds((hx, hy, hz)), sds((qx * qy, qz)), sds((slots, cells))),
        in_specs=[SMEM] * 2 + [VMEM] * 5,
        out_specs=(VMEM,) * 3,
        scratch_shapes=[
            pltpu.VMEM((ex, ey, hz), F32),
            pltpu.VMEM((ex, ey, hz), F32),
            pltpu.VMEM((9, ex, ey, hz), F32),
            pltpu.VMEM((hx // 2 * ey, hz), F32),
        ],
        flops=20_000_000,
    )(flags, places, fx, *fy, d_wide, w_wide)

    arrived = lax.all_to_all(outgoing, "dev", split_axis=0, concat_axis=0, tiled=True)
    owned = call(solve_blocks, sds((slots, cells)), in_specs=[VMEM] * 2, out_specs=VMEM)(
        inverse_blocks.reshape(slots, cells, cells), arrived
    )
    returned = lax.all_to_all(owned, "dev", split_axis=0, concat_axis=0, tiled=True)
    correction, residual = call(
        finish,
        (sds((qx, qy, qz)), sds((qx, qy, qz))),
        in_specs=[SMEM] + [VMEM] * 4,
        out_specs=(VMEM,) * 2,
        scratch_shapes=[pltpu.VMEM((owners.shape[0], cells), F32)],
    )(
        places,
        returned,
        source,
        diag_coarse.reshape(qx * qy, qz),
        coup_coarse.reshape(26, qx * qy, qz),
    )
    return fine_iterate, mid_iterate, correction, residual


def solution(mesh):
    return jax.shard_map(
        shards,
        mesh=mesh,
        in_specs=(
            P("group", "dev", None),
            P("group", "dev", None),
            P(None, "group", "dev", None),
            P("group", "dev", None),
            P(None, "group", "dev", None),
            P("group", "dev", None),
            P(None, "group", "dev", None),
            P("group", "dev", None, None),
            P("group", "dev", None, None, None),
        ),
        out_specs=(
            P("group", "dev", None),
            P("group", "dev", None),
            P("group", "dev", None),
            P("group", "dev", None),
        ),
        check_vma=False,
    )
```
